32 devices in a mesh: ctx: 8 (over z, core), fsdp: 4 (over y, x).
Axes of the slice: x: 2, y: 2, z: 4, core: 2. Of those that a mesh axis runs over, the one named last changes fastest.
Arguments:
- tokens: bfloat16 [4096, 8192], P('ctx', 'fsdp'), may hold values from -6 to 6
- gain: float32 [8192], replicated, may hold values from 0.5 to 1.5
- in_weight: bfloat16 [8192, 3, 4096], P('ctx', None, 'fsdp'), may hold values from -0.0625 to 0.0625
- short_filter: float32 [3, 3, 4096], P(None, None, 'fsdp'), may hold values from -3.5 to 3.5
- long_filter: float32 [128, 4096], P(None, 'fsdp'), may hold values from -0.5 to 0.5
Outputs:
- gated_out: bfloat16 [4096, 4096], P('ctx', 'fsdp')
The draws below stay inside these ranges and needn't reach their ends.
All inputs are finite; a program needn't handle non-finite values.
Results may differ from the reference program's by a relative error of at most 0.0086.
Values may be sent and summed in bfloat16 or wider, within the bound.
No kernel may reach another device: no remote copies, remote signals or barrier semaphores. Data moves between devices by JAX's collectives and lax.ppermute only.
A program may use at most 128 MiB of HBM per device.

```python
import jax
import jax.numpy as jnp
from jax import lax

D = 8192
FILT = 128
SHORT = 3
CH = 4096
TOKENS = 4096


def block_scale(key, dims, shards, low, largest):
    loudness, own = 1.0, jax.random.fold_in(key, 6)
    for axis_at, shards_of in shards:
        heights = jnp.exp(jax.random.uniform(jax.random.fold_in(own, axis_at), (shards_of,), jnp.float32, low / len(shards), largest / len(shards)))
        loudness = loudness * jnp.repeat(heights, dims[axis_at] // shards_of).reshape([-1 if axis == axis_at else 1 for axis in range(len(dims))])
    return loudness


def scatter_about(rng, extent, deviation, reach, cuts=(), held_as=jnp.bfloat16):
    array = jax.random.normal(rng, extent, jnp.float32) * deviation
    if len(cuts) > 0:
        array = block_scale(rng, extent, cuts, -0.22, 0.18) * array
    return jnp.clip(array, min=-reach, max=reach).astype(held_as)


def setup_inputs(seed: int = 0) -> dict:
    splits = jax.random.split(jax.random.key(seed), 6)
    return {
        "tokens": scatter_about(splits[0], (TOKENS, D), 1.0, 6.0, ((0, 8), (1, 4))),
        "gain": jnp.clip(1.0 + 0.1 * jax.random.normal(splits[1], (D,), jnp.float32), 0.5, 1.5),
        "in_weight": scatter_about(splits[2], (D, 3, CH), D ** -0.5, 0.0625, ((0, 8), (2, 4))),
        "short_filter": scatter_about(splits[3], (SHORT, 3, CH), SHORT ** -0.5, 3.5, ((2, 4),), jnp.float32),
        "long_filter": scatter_about(splits[4], (FILT, CH), FILT ** -0.5, 0.5, ((1, 4),), jnp.float32),
    }


def reference(tokens, gain, in_weight, short_filter, long_filter):
    widened = tokens.astype(jnp.float32)
    mean_square = lax.optimization_barrier(jnp.mean(widened * widened, axis=1, keepdims=True))
    normed = (widened * lax.rsqrt(mean_square + 1e-06) * gain).astype(jnp.bfloat16)
    total_rows = tokens.shape[0]
    channels = in_weight.shape[2]
    projected = jnp.dot(normed, in_weight.reshape(in_weight.shape[0], 3 * channels), preferred_element_type=jnp.float32).astype(jnp.bfloat16)
    short_taps = short_filter.reshape(SHORT, 3 * channels)
    padded = jnp.concatenate([jnp.zeros((SHORT - 1, 3 * channels), jnp.float32), projected.astype(jnp.float32)], axis=0)
    featurized = jnp.zeros((total_rows, 3 * channels), jnp.float32)
    for offset in range(SHORT):
        featurized = featurized + short_taps[offset] * padded[SHORT - 1 - offset:SHORT - 1 - offset + total_rows]
    query = featurized[:, :channels]
    keyed = featurized[:, channels:2 * channels]
    valued = featurized[:, 2 * channels:]
    gated = (keyed * valued).astype(jnp.bfloat16)
    signal = jnp.concatenate([jnp.zeros((FILT - 1, channels), jnp.float32), gated.astype(jnp.float32)], axis=0)
    response = jnp.zeros((total_rows, channels), jnp.float32)
    for offset in range(FILT):
        response = response + long_filter[offset] * signal[FILT - 1 - offset:FILT - 1 - offset + total_rows]
    return (query * response).astype(jnp.bfloat16)
```

```python
import jax
import jax.numpy as jnp
import numpy as np
from jax import lax
from jax.sharding import PartitionSpec as P

CORES = 2
STAGES = 4
EPS = 1e-06


def pick(stack, index):
    return lax.dynamic_index_in_dim(stack, index, 0, keepdims=False)


def swap(value, count, bits):
    if bits == 0:
        return value
    return lax.ppermute(value, "fsdp", [(j, j ^ bits) for j in range(count)])


def plane_shift(value, edges):
    return lax.ppermute(
        value, "ctx", [(a * CORES + c, b * CORES + c) for a, b in edges for c in range(CORES)]
    )


def line_sum(partials):
    planes = len(partials)
    right, left = None, None

    def onward(term, arrived):
        if arrived is not None:
            term = term + arrived.astype(jnp.float32)
        return term.astype(jnp.bfloat16)

    for step in range(1, planes):
        right = plane_shift(
            onward(partials[planes - step], right),
            [(p, p + 1) for p in range(planes - 1) if p < step],
        )
        left = plane_shift(
            onward(partials[step], left),
            [(p, p - 1) for p in range(1, planes) if p >= planes - step],
        )
    return partials[0] + right.astype(jnp.float32) + left.astype(jnp.float32)


def dft_matrices(length, taps):
    bins = length // 2 + 1
    k = np.arange(bins)[:, None]
    angle = 2.0 * np.pi * ((k * np.arange(length)[None, :]) % length) / length
    weight = np.where((k == 0) | (k == length // 2), 1.0, 2.0) / length
    analysis = np.stack([np.cos(angle), -np.sin(angle)])
    synthesis = np.stack([weight * np.cos(angle), -weight * np.sin(angle)])
    return analysis.astype(np.float32), synthesis[:, :, taps:].astype(np.float32)


def long_mix(signal, filters, row_count):
    taps = filters.shape[0]
    length = 2 * taps
    blocks = row_count // taps
    analysis, synthesis = dft_matrices(length, taps)
    pieces = jnp.stack([signal[b * taps : b * taps + length] for b in range(blocks)])
    pieces = pieces.astype(jnp.float32)
    high = lax.Precision.HIGH
    spectrum = jnp.einsum("pkn,bnc->pbkc", analysis, pieces, precision=high)
    tones = jnp.einsum("pkn,nc->pkc", analysis[:, :, :taps], filters, precision=high)
    real = spectrum[0] * tones[0] - spectrum[1] * tones[1]
    imag = spectrum[0] * tones[1] + spectrum[1] * tones[0]
    result = jnp.einsum("kn,bkc->bnc", synthesis[0], real, precision=high) + jnp.einsum(
        "kn,bkc->bnc", synthesis[1], imag, precision=high
    )
    return result.reshape(row_count, -1)


def on_device(tokens, gain, in_weight, short_filter, long_filter):
    planes = lax.axis_size("ctx") // CORES
    columns = lax.axis_size("fsdp")
    plane = lax.axis_index("ctx") // CORES
    column = lax.axis_index("fsdp")
    row_count, width = tokens.shape
    channels = in_weight.shape[2]

    pairs = [[p * CORES + c for c in range(CORES)] for p in range(planes)]
    weight = lax.all_gather(in_weight, "ctx", axis=0, tiled=True, axis_index_groups=pairs)
    weight = weight.reshape(weight.shape[0], 3 * channels)
    gains = gain.reshape(columns, width)

    stage_rows = row_count // STAGES
    share = stage_rows // columns
    projected = []
    for stage in range(STAGES):
        own = tokens[stage * stage_rows : (stage + 1) * stage_rows].reshape(columns, share, width)
        wide = jnp.stack([swap(pick(own, column ^ t), columns, t) for t in range(columns)])
        wide = wide.astype(jnp.float32)
        mean_square = jnp.sum(wide * wide, axis=(0, 2), keepdims=True) / (columns * width)
        gain_here = jnp.stack([pick(gains, column ^ t) for t in range(columns)])
        normed = wide * lax.rsqrt(mean_square + EPS) * gain_here[:, None, :]
        normed = normed.astype(jnp.bfloat16)
        rows_of = [None] * planes
        for d in range(planes):
            piece = pick(normed, column ^ ((plane + d) % planes))
            if d > 0:
                piece = plane_shift(piece, [(p, (p + d) % planes) for p in range(planes)])
            rows_of[(planes - d) % planes] = piece
        mine = jnp.stack(rows_of)
        lhs = jnp.stack([swap(mine, columns, t) for t in range(columns)], axis=1)
        partial = jnp.dot(
            lhs.reshape(planes * stage_rows, -1), weight, preferred_element_type=jnp.float32
        ).reshape(planes, stage_rows, 3 * channels)
        total = line_sum([partial[m] for m in range(planes)])
        total = total.astype(jnp.bfloat16).reshape(columns, share, 3 * channels)
        projected += [pick(total, column ^ t) for t in range(columns)]
    projected = jnp.concatenate(projected, axis=0)

    short_taps = short_filter.reshape(short_filter.shape[0], 3 * channels)
    short_count, long_count = short_taps.shape[0], long_filter.shape[0]
    edge = short_count - 1

    def short_mix(extended, taps, count):
        extended = extended.astype(jnp.float32)
        result = taps[0] * extended[edge : edge + count]
        for offset in range(1, short_count):
            result = result + taps[offset] * extended[edge - offset : edge - offset + count]
        return result

    def gate(mixed):
        return (mixed[:, channels : 2 * channels] * mixed[:, 2 * channels :]).astype(jnp.bfloat16)

    shards = lax.axis_size("ctx")
    onward = [(i, i + 1) for i in range(shards - 1)]
    last = gate(short_mix(projected[row_count - long_count - edge :], short_taps, long_count))
    upper_rim = lax.ppermute(projected[row_count - edge :], "ctx", onward)
    gated_rim = lax.ppermute(last, "ctx", onward)
    featurized = short_mix(jnp.concatenate([upper_rim, projected], axis=0), short_taps, row_count)
    signal = jnp.concatenate([gated_rim, gate(featurized)], axis=0)
    response = long_mix(signal, long_filter, row_count)
    return (featurized[:, :channels] * response).astype(jnp.bfloat16)


def solution(mesh):
    return jax.shard_map(
        on_device,
        mesh=mesh,
        in_specs=(
            P("ctx", "fsdp"),
            P(),
            P("ctx", None, "fsdp"),
            P(None, None, "fsdp"),
            P(None, "fsdp"),
        ),
        out_specs=P("ctx", "fsdp"),
        check_vma=False,
    )
```

```python
import jax
import jax.numpy as jnp
import numpy as np
from jax import lax
from jax.experimental import pallas as pl
from jax.experimental.pallas import tpu as pltpu
from jax.sharding import PartitionSpec as P

CORES = 2
EPS = 1e-06
STAGES = (3, 5)
ROUNDS = (((0, 0), (1, 1), (2, 2), (3, 3), 4), ((1, 1), (2, 3), (4, 4), (5, 5), 6))
LANES = 128


def pick(stack, index):
    return lax.dynamic_index_in_dim(stack, index, 0, keepdims=False)


def swap(value, count, bits):
    if bits == 0:
        return value
    return lax.ppermute(value, "fsdp", [(j, j ^ bits) for j in range(count)])


def plane_shift(value, edges):
    return lax.ppermute(
        value, "ctx", [(a * CORES + c, b * CORES + c) for a, b in edges for c in range(CORES)]
    )


def dft_matrices(length, taps):
    bins = length // 2 + 1
    room = -(-bins // 8) * 8
    k = np.arange(bins)[:, None]
    angle = 2.0 * np.pi * ((k * np.arange(length)[None, :]) % length) / length
    weight = np.where((k == 0) | (k == length // 2), 1.0, 2.0) / length
    analysis = np.zeros((2, room, length))
    synthesis = np.zeros((2, room, length))
    analysis[:, :bins] = np.stack([np.cos(angle), -np.sin(angle)])
    synthesis[:, :bins] = np.stack([weight * np.cos(angle), -weight * np.sin(angle)])
    return (
        analysis.reshape(2 * room, length).astype(np.float32),
        synthesis.reshape(2 * room, length)[:, taps:].T.astype(np.float32),
    )


def tile(*extents):
    return 2 * LANES if all(e % (2 * LANES) == 0 for e in extents) else LANES


def halves(value):
    high = value.astype(jnp.bfloat16)
    return high, (value - high.astype(jnp.float32)).astype(jnp.bfloat16)


def dot(a, b):
    return jnp.dot(a, b, preferred_element_type=jnp.float32)


def finish_kernel(
    query, key, value, query_rim, key_rim, value_rim, gated_rim, short, long,
    analysis_high, analysis_low, synthesis_high, synthesis_low, out, extended, signal,
):
    row_count = out.shape[0]
    taps = long.shape[0]
    room = analysis_high.shape[0] // 2
    reach = short.shape[0]
    for b, (body, rim) in enumerate(((query, query_rim), (key, key_rim), (value, value_rim))):
        extended[b, :8] = rim[rim.shape[0] - 8 :].astype(jnp.float32)
        extended[b, 8:] = body[...].astype(jnp.float32)

    def featurized(b, start, count):
        result = None
        for s in range(reach):
            term = short[s, b : b + 1, :] * extended[b, 8 + start - s : 8 + start - s + count]
            result = term if result is None else result + term
        return result

    signal[:taps] = gated_rim[...]
    for start in range(0, row_count, taps):
        gated = featurized(1, start, taps) * featurized(2, start, taps)
        signal[taps + start : 2 * taps + start] = gated.astype(jnp.bfloat16)

    long_high, long_low = halves(long[...])
    tones = (
        dot(analysis_high[:, :taps], long_high)
        + dot(analysis_high[:, :taps], long_low)
        + dot(analysis_low[:, :taps], long_high)
    )
    for start in range(0, row_count, taps):
        block = signal[start : start + 2 * taps]
        spectrum = dot(analysis_high[...], block) + dot(analysis_low[...], block)
        real = spectrum[:room] * tones[:room] - spectrum[room:] * tones[room:]
        imag = spectrum[:room] * tones[room:] + spectrum[room:] * tones[:room]
        high, low = halves(jnp.concatenate([real, imag], axis=0))
        response = (
            dot(synthesis_high[...], high)
            + dot(synthesis_high[...], low)
            + dot(synthesis_low[...], high)
        )
        out[start : start + taps] = (featurized(0, start, taps) * response).astype(out.dtype)


def finish(projected, rim, gated_rim, short_filter, long_filter):
    row_count = projected.shape[0]
    taps, channels = long_filter.shape
    width = tile(channels)
    count = channels // width
    analysis, synthesis = (jnp.asarray(m) for m in dft_matrices(2 * taps, taps))
    constants = (*halves(analysis), *halves(synthesis))

    def branch(rows, b):
        return pl.BlockSpec((rows, width), lambda i, b=b: (0, b * count + i))

    operands = [*[projected] * 3, *[rim] * 3, gated_rim, short_filter, long_filter, *constants]
    specs = (
        [branch(row_count, b) for b in range(3)]
        + [branch(rim.shape[0], b) for b in range(3)]
        + [
            pl.BlockSpec((taps, width), lambda i: (0, i)),
            pl.BlockSpec((short_filter.shape[0], 3, width), lambda i: (0, 0, i)),
            pl.BlockSpec((taps, width), lambda i: (0, i)),
        ]
        + [pl.BlockSpec(m.shape, lambda i: (0, 0)) for m in constants]
    )
    return pl.pallas_call(
        finish_kernel,
        out_shape=jax.ShapeDtypeStruct((row_count, channels), jnp.bfloat16),
        grid=(count,),
        in_specs=specs,
        out_specs=pl.BlockSpec((row_count, width), lambda i: (0, i)),
        scratch_shapes=[
            pltpu.VMEM((3, 8 + row_count, width), jnp.float32),
            pltpu.VMEM((taps + row_count, width), jnp.bfloat16),
        ],
        compiler_params=pltpu.CompilerParams(vmem_limit_bytes=32 * 1024 * 1024),
        cost_estimate=pl.CostEstimate(
            flops=row_count * channels * 5000, bytes_accessed=row_count * channels * 10, transcendentals=0
        ),
    )(*operands)


def passed_along(value):
    count = lax.axis_size("ctx")
    return lax.ppermute(value, "ctx", [(i, i + 1) for i in range(count - 1)])


def rims(last_rows, short_filter, long_count):
    reach = short_filter.shape[0]
    channels = short_filter.shape[2]
    total = last_rows.shape[0]
    mixed = []
    for b in (1, 2):
        rows = last_rows[:, b * channels : (b + 1) * channels].astype(jnp.float32)
        mixed.append(
            sum(
                short_filter[s, b] * rows[total - long_count - s : total - s] for s in range(reach)
            )
        )
    gated = (mixed[0] * mixed[1]).astype(jnp.bfloat16)
    return passed_along(last_rows[total - 16 :]), passed_along(gated)


def together(values):
    leaves, tree = jax.tree.flatten(values)
    anywhere = pl.BlockSpec(memory_space=pl.ANY)
    leaves = pl.pallas_call(
        lambda *refs: None,
        out_shape=[jax.ShapeDtypeStruct(leaf.shape, leaf.dtype) for leaf in leaves],
        in_specs=[anywhere] * len(leaves),
        out_specs=[anywhere] * len(leaves),
        input_output_aliases={at: at for at in range(len(leaves))},
    )(*leaves)
    return jax.tree.unflatten(tree, leaves)


def spread_near(value, columns):
    if columns != 4:
        return [swap(value, columns, t) for t in range(1, columns)]
    return [swap(value, columns, 1), swap(value, columns, 2)]


def spread_far(near, columns):
    if columns != 4:
        return []
    half = near[0].shape[-1] // 2
    return [swap(near[1][..., :half], columns, 1), swap(near[0][..., half:], columns, 2)]


def spread_all(value, near, far):
    return [value, *near] + ([jnp.concatenate(far, axis=-1)] if far else [])


def partial_kernel(column, *refs):
    *lefts, own, other, out, joined = refs
    planes, columns, share, depth = joined.shape

    @pl.when(pl.program_id(0) == 0)
    def _():
        for t, left in enumerate(lefts):
            joined[:, column[0] ^ t] = left[...]

    rows = joined[...].reshape(planes * columns * share, depth)
    half = depth // 2
    out[...] = dot(rows[:, :half], own[0]) + dot(rows[:, half:], other[0])


def partial_sums(column, lefts, part, parts, own, other):
    planes, share, depth = lefts[0].shape
    planes = planes // parts
    columns = len(lefts)
    late = own.shape[2]
    rows = planes * columns * share
    weights = pl.BlockSpec((1, own.shape[1], late), lambda b, _: (b, 0, 0))
    return pl.pallas_call(
        partial_kernel,
        out_shape=jax.ShapeDtypeStruct((rows, 3 * late), jnp.float32),
        grid_spec=pltpu.PrefetchScalarGridSpec(
            num_scalar_prefetch=1,
            grid=(3,),
            in_specs=[pl.BlockSpec((planes, share, depth), lambda b, _: (part, 0, 0))] * columns
            + [weights, weights],
            out_specs=pl.BlockSpec((rows, late), lambda b, _: (0, b)),
            scratch_shapes=[pltpu.VMEM((planes, columns, share, depth), jnp.bfloat16)],
        ),
        compiler_params=pltpu.CompilerParams(vmem_limit_bytes=48 * 1024 * 1024),
        cost_estimate=pl.CostEstimate(
            flops=2 * rows * depth * 3 * late,
            bytes_accessed=2 * rows * depth + 6 * depth * late + 12 * rows * late,
            transcendentals=0,
        ),
    )(column, *lefts, own, other).reshape(planes, columns * share, 3 * late)


def on_device(tokens, gain, in_weight, short_filter, long_filter):
    planes = lax.axis_size("ctx") // CORES
    columns = lax.axis_size("fsdp")
    plane = lax.axis_index("ctx") // CORES
    core = lax.axis_index("ctx") % CORES
    column = lax.axis_index("fsdp")
    place = jnp.stack([column, plane]).astype(jnp.int32)
    row_count, width = tokens.shape
    long_count = long_filter.shape[0]

    parts = STAGES
    if row_count % (sum(parts) * columns * 16):
        parts = (1, 1)
    unit = row_count // sum(parts)
    sizes = [unit * part for part in parts]
    stages = [(row_count - sizes[0], sizes[0]), (0, sizes[1])]

    own_weight = jnp.transpose(in_weight, (1, 0, 2))
    other_weight = lax.ppermute(
        own_weight,
        "ctx",
        [(p * CORES + c, p * CORES + 1 - c) for p in range(planes) for c in range(CORES)],
    )
    gains = gain.reshape(columns, width)
    gain_here = jnp.stack([pick(gains, column ^ t) for t in range(columns)])[:, None, :]

    def to_trade(stage):
        start, size = stages[stage]
        own = tokens[start : start + size].reshape(columns, -1, width)
        return [pick(own, column ^ t) for t in range(columns)]

    def trade(pieces):
        return [swap(piece, columns, t) for t, piece in enumerate(pieces)]

    def normalize(wide):
        wide = jnp.stack(wide).astype(jnp.float32)
        mean_square = jnp.sum(wide * wide, axis=(0, 2), keepdims=True) / (columns * width)
        return (wide * lax.rsqrt(mean_square + EPS) * gain_here).astype(jnp.bfloat16)

    def turned(normed):
        return jnp.where(core == 0, normed, jnp.roll(normed, width // 2, axis=2))

    def to_planes(normed):
        rows_of = [None] * planes
        for d in range(planes):
            piece = pick(normed, column ^ ((plane + d) % planes))
            if d > 0:
                piece = plane_shift(piece, [(p, (p + d) % planes) for p in range(planes)])
            rows_of[(planes - d) % planes] = piece
        return rows_of

    def send_weights(step, right, left):
        return (
            plane_shift(right, [(p, p + 1) for p in range(planes - 1) if p >= step - 1]),
            plane_shift(left, [(p, p - 1) for p in range(1, planes) if p <= planes - step]),
        )

    def onward(term, arrived):
        if arrived is not None:
            term = term + arrived.astype(jnp.float32)
        return term.astype(jnp.bfloat16)

    def send_sums(step, terms, sums):
        right, left = sums
        return (
            plane_shift(
                onward(terms[planes - step], right),
                [(p, p + 1) for p in range(planes - 1) if p < step],
            ),
            plane_shift(
                onward(terms[step], left),
                [(p, p - 1) for p in range(1, planes) if p >= planes - step],
            ),
        )

    count, steps = len(stages), planes - 1
    order = [m for k in range(1, planes // 2) for m in (planes - k, k)] + [planes // 2, 0]
    last = max(at[4] for at in ROUNDS) + steps - 1
    live = {f"pieces{stage}": to_trade(stage) for stage in range(count)}
    own, normed, terms, totals, flying = {}, {}, {}, {}, {}

    for now in range(last + 1):
        for stage, (to_shares, across, near, far, first) in enumerate(ROUNDS):
            if now == to_shares[0]:
                flying[f"trade{stage}"] = to_shares[1], trade(live.pop(f"pieces{stage}"))
            if now == across[0]:
                normed[stage] = turned(normalize(live.pop(f"trade{stage}")))
                flying[f"planes{stage}"] = across[1], to_planes(normed[stage])
            if now == near[0]:
                pieces = live.pop(f"planes{stage}")
                own[stage] = jnp.stack([pieces[m] for m in order])
                flying[f"near{stage}"] = near[1], spread_near(own[stage], columns)
            if now == far[0]:
                flying[f"far{stage}"] = far[1], spread_far(live[f"near{stage}"], columns)
            if now == first:
                lefts = spread_all(
                    own[stage], live.pop(f"near{stage}"), live.pop(f"far{stage}")
                )
                products = [
                    product[m]
                    for half in range(2)
                    for product in [
                        partial_sums(place, lefts, half, 2, own_weight, other_weight)
                    ]
                    for m in range(planes // 2)
                ]
                terms[stage] = [products[order.index(m)] for m in range(planes)]
                live[f"sums{stage}"] = (None, None)
            if first <= now < first + steps:
                sums = live.pop(f"sums{stage}")
                flying[f"sums{stage}"] = now, send_sums(now - first + 1, terms[stage], sums)
        for name in [name for name, (end, _) in flying.items() if end == now]:
            live[name] = flying.pop(name)[1]
        live = together(live) if now < last else live
        for stage in range(count):
            if now == ROUNDS[stage][4] + steps - 1:
                right, left = live.pop(f"sums{stage}")
                total = terms[stage][0] + right.astype(jnp.float32) + left.astype(jnp.float32)
                totals[stage] = total.astype(jnp.bfloat16)

    rim, gated_rim = rims(totals[0], short_filter, long_count)
    projected = jnp.concatenate([totals[1], totals[0]], axis=0)
    return finish(projected, rim, gated_rim, short_filter, long_filter)


def solution(mesh):
    return jax.shard_map(
        on_device,
        mesh=mesh,
        in_specs=(
            P("ctx", "fsdp"),
            P(),
            P("ctx", None, "fsdp"),
            P(None, None, "fsdp"),
            P(None, "fsdp"),
        ),
        out_specs=P("ctx", "fsdp"),
        check_vma=False,
    )
```

```python
import jax
import jax.numpy as jnp
import numpy as np
from jax import lax
from jax.experimental import pallas as pl
from jax.experimental.pallas import tpu as pltpu
from jax.sharding import PartitionSpec as P

CORES = 2
EPS = 1e-06
STAGES = (3, 5)
ROUNDS = ((0, (1, 1), 2, 3, 4, 4), (1, (2, 3), 4, 5, 6, 7))
CHAINS = (1, 2)
LANES = 128


def pick(stack, index):
    return lax.dynamic_index_in_dim(stack, index, 0, keepdims=False)


def swap(value, count, bits):
    if bits == 0:
        return value
    return lax.ppermute(value, "fsdp", [(j, j ^ bits) for j in range(count)])


def plane_shift(value, edges):
    return lax.ppermute(
        value, "ctx", [(a * CORES + c, b * CORES + c) for a, b in edges for c in range(CORES)]
    )


def dft_matrices(length, taps):
    bins = length // 2 + 1
    room = -(-bins // 8) * 8
    k = np.arange(bins)[:, None]
    angle = 2.0 * np.pi * ((k * np.arange(length)[None, :]) % length) / length
    weight = np.where((k == 0) | (k == length // 2), 1.0, 2.0) / length
    analysis = np.zeros((2, room, length))
    synthesis = np.zeros((2, room, length))
    analysis[:, :bins] = np.stack([np.cos(angle), -np.sin(angle)])
    synthesis[:, :bins] = np.stack([weight * np.cos(angle), -weight * np.sin(angle)])
    return (
        analysis.reshape(2 * room, length).astype(np.float32),
        synthesis.reshape(2 * room, length)[:, taps:].T.astype(np.float32),
    )


def tile(*extents):
    return 2 * LANES if all(e % (2 * LANES) == 0 for e in extents) else LANES


def halves(value):
    high = value.astype(jnp.bfloat16)
    return high, (value - high.astype(jnp.float32)).astype(jnp.bfloat16)


def dot(a, b):
    return jnp.dot(a, b, preferred_element_type=jnp.float32)


def finish_kernel(
    query, key, value, query_rim, key_rim, value_rim, gated_rim, short, long,
    analysis_high, analysis_low, synthesis_high, synthesis_low, out, extended, signal,
):
    row_count = out.shape[0]
    taps = long.shape[0]
    room = analysis_high.shape[0] // 2
    reach = short.shape[0]
    for b, (body, rim) in enumerate(((query, query_rim), (key, key_rim), (value, value_rim))):
        extended[b, :8] = rim[rim.shape[0] - 8 :].astype(jnp.float32)
        extended[b, 8:] = body[...].astype(jnp.float32)

    def featurized(b, start, count):
        result = None
        for s in range(reach):
            term = short[s, b : b + 1, :] * extended[b, 8 + start - s : 8 + start - s + count]
            result = term if result is None else result + term
        return result

    signal[:taps] = gated_rim[...]
    for start in range(0, row_count, taps):
        gated = featurized(1, start, taps) * featurized(2, start, taps)
        signal[taps + start : 2 * taps + start] = gated.astype(jnp.bfloat16)

    long_high, long_low = halves(long[...])
    tones = (
        dot(analysis_high[:, :taps], long_high)
        + dot(analysis_high[:, :taps], long_low)
        + dot(analysis_low[:, :taps], long_high)
    )
    for start in range(0, row_count, taps):
        block = signal[start : start + 2 * taps]
        spectrum = dot(analysis_high[...], block) + dot(analysis_low[...], block)
        real = spectrum[:room] * tones[:room] - spectrum[room:] * tones[room:]
        imag = spectrum[:room] * tones[room:] + spectrum[room:] * tones[:room]
        high, low = halves(jnp.concatenate([real, imag], axis=0))
        response = (
            dot(synthesis_high[...], high)
            + dot(synthesis_high[...], low)
            + dot(synthesis_low[...], high)
        )
        out[start : start + taps] = (featurized(0, start, taps) * response).astype(out.dtype)


def finish(projected, rim, gated_rim, short_filter, long_filter):
    row_count = projected.shape[0]
    taps, channels = long_filter.shape
    width = tile(channels)
    count = channels // width
    analysis, synthesis = (jnp.asarray(m) for m in dft_matrices(2 * taps, taps))
    constants = (*halves(analysis), *halves(synthesis))

    def branch(rows, b):
        return pl.BlockSpec((rows, width), lambda i, b=b: (0, b * count + i))

    operands = [*[projected] * 3, *[rim] * 3, gated_rim, short_filter, long_filter, *constants]
    specs = (
        [branch(row_count, b) for b in range(3)]
        + [branch(rim.shape[0], b) for b in range(3)]
        + [
            pl.BlockSpec((taps, width), lambda i: (0, i)),
            pl.BlockSpec((short_filter.shape[0], 3, width), lambda i: (0, 0, i)),
            pl.BlockSpec((taps, width), lambda i: (0, i)),
        ]
        + [pl.BlockSpec(m.shape, lambda i: (0, 0)) for m in constants]
    )
    return pl.pallas_call(
        finish_kernel,
        out_shape=jax.ShapeDtypeStruct((row_count, channels), jnp.bfloat16),
        grid=(count,),
        in_specs=specs,
        out_specs=pl.BlockSpec((row_count, width), lambda i: (0, i)),
        scratch_shapes=[
            pltpu.VMEM((3, 8 + row_count, width), jnp.float32),
            pltpu.VMEM((taps + row_count, width), jnp.bfloat16),
        ],
        compiler_params=pltpu.CompilerParams(vmem_limit_bytes=32 * 1024 * 1024),
        cost_estimate=pl.CostEstimate(
            flops=row_count * channels * 5000, bytes_accessed=row_count * channels * 10, transcendentals=0
        ),
    )(*operands)


def passed_along(value):
    count = lax.axis_size("ctx")
    return lax.ppermute(value, "ctx", [(i, i + 1) for i in range(count - 1)])


def rims(last_rows, short_filter, long_count):
    reach = short_filter.shape[0]
    channels = short_filter.shape[2]
    total = last_rows.shape[0]
    mixed = []
    for b in (1, 2):
        rows = last_rows[:, b * channels : (b + 1) * channels].astype(jnp.float32)
        mixed.append(
            sum(
                short_filter[s, b] * rows[total - long_count - s : total - s] for s in range(reach)
            )
        )
    gated = (mixed[0] * mixed[1]).astype(jnp.bfloat16)
    return passed_along(last_rows[total - 16 :]), passed_along(gated)


def together(values):
    leaves, tree = jax.tree.flatten(values)
    anywhere = pl.BlockSpec(memory_space=pl.ANY)
    leaves = pl.pallas_call(
        lambda *refs: None,
        out_shape=[jax.ShapeDtypeStruct(leaf.shape, leaf.dtype) for leaf in leaves],
        in_specs=[anywhere] * len(leaves),
        out_specs=[anywhere] * len(leaves),
        input_output_aliases={at: at for at in range(len(leaves))},
    )(*leaves)
    return jax.tree.unflatten(tree, leaves)


def spread_near(value, columns):
    if columns != 4:
        return [swap(value, columns, t) for t in range(1, columns)]
    return [swap(value, columns, 1), swap(value, columns, 2)]


def spread_far(near, columns):
    if columns != 4:
        return []
    half = near[0].shape[-1] // 2
    return [swap(near[1][..., :half], columns, 1), swap(near[0][..., half:], columns, 2)]


def spread_all(value, near, far):
    return [value, *near] + ([jnp.concatenate(far, axis=-1)] if far else [])


def partial_kernel(column, *refs):
    own, other, out, joined = refs[-4:]
    planes, columns, share, depth = joined.shape
    lefts = refs[:columns]

    @pl.when(pl.program_id(0) == 0)
    def _():
        for t, left in enumerate(lefts):
            joined[:, column[0] ^ t] = left[...]

    rows = joined[...].reshape(planes * columns * share, depth)
    half = depth // 2
    total = dot(rows[:, :half], own[0]) + dot(rows[:, half:], other[0])
    out[...] = total.astype(out.dtype)


def partial_sums(column, lefts, part, parts, own, other):
    planes, share, depth = lefts[0].shape
    planes = planes // parts
    columns = len(lefts)
    late = own.shape[2]
    rows = planes * columns * share
    weights = pl.BlockSpec((1, own.shape[1], late), lambda b, _: (b, 0, 0))
    return pl.pallas_call(
        partial_kernel,
        out_shape=jax.ShapeDtypeStruct((rows, 3 * late), jnp.bfloat16),
        grid_spec=pltpu.PrefetchScalarGridSpec(
            num_scalar_prefetch=1,
            grid=(3,),
            in_specs=[pl.BlockSpec((planes, share, depth), lambda b, _: (part, 0, 0))] * columns
            + [weights, weights],
            out_specs=pl.BlockSpec((rows, late), lambda b, _: (0, b)),
            scratch_shapes=[pltpu.VMEM((planes, columns, share, depth), jnp.bfloat16)],
        ),
        compiler_params=pltpu.CompilerParams(vmem_limit_bytes=48 * 1024 * 1024),
        cost_estimate=pl.CostEstimate(
            flops=2 * rows * depth * 3 * late,
            bytes_accessed=2 * rows * depth + 6 * depth * late + 6 * rows * late,
            transcendentals=0,
        ),
    )(column, *lefts, own, other).reshape(planes, columns * share, 3 * late)


def on_device(tokens, gain, in_weight, short_filter, long_filter):
    planes = lax.axis_size("ctx") // CORES
    columns = lax.axis_size("fsdp")
    plane = lax.axis_index("ctx") // CORES
    core = lax.axis_index("ctx") % CORES
    column = lax.axis_index("fsdp")
    place = jnp.stack([column, plane]).astype(jnp.int32)
    row_count, width = tokens.shape
    long_count = long_filter.shape[0]

    parts = STAGES
    if row_count % (sum(parts) * columns * 16):
        parts = (1, 1)
    unit = row_count // sum(parts)
    sizes = [unit * part for part in parts]
    stages = [(row_count - sizes[0], sizes[0]), (0, sizes[1])]

    own_weight = jnp.transpose(in_weight, (1, 0, 2))
    other_weight = lax.ppermute(
        own_weight,
        "ctx",
        [(p * CORES + c, p * CORES + 1 - c) for p in range(planes) for c in range(CORES)],
    )
    gains = gain.reshape(columns, width)
    gain_here = jnp.stack([pick(gains, column ^ t) for t in range(columns)])[:, None, :]

    def to_trade(stage):
        start, size = stages[stage]
        own = tokens[start : start + size].reshape(columns, -1, width)
        return [pick(own, column ^ t) for t in range(columns)]

    def trade(pieces):
        return [swap(piece, columns, t) for t, piece in enumerate(pieces)]

    def normalize(wide):
        wide = jnp.stack(wide).astype(jnp.float32)
        mean_square = jnp.sum(wide * wide, axis=(0, 2), keepdims=True) / (columns * width)
        return (wide * lax.rsqrt(mean_square + EPS) * gain_here).astype(jnp.bfloat16)

    def turned(normed):
        return jnp.where(core == 0, normed, jnp.roll(normed, width // 2, axis=2))

    def to_planes(normed, distances):
        rows_of = {}
        for d in distances:
            piece = pick(normed, column ^ ((plane + d) % planes))
            rows_of[planes - d] = plane_shift(piece, [(p, (p + d) % planes) for p in range(planes)])
        return rows_of

    def onward(step, terms, sums):
        sent = terms[planes - step], terms[step]
        if sums is None:
            return sent
        return [
            (term.astype(jnp.float32) + arrived.astype(jnp.float32)).astype(jnp.bfloat16)
            for term, arrived in zip(sent, sums)
        ]

    def send_sums(step, right, left):
        return (
            plane_shift(right, [(p, p + 1) for p in range(planes - 1) if p < step]),
            plane_shift(left, [(p, p - 1) for p in range(1, planes) if p >= planes - step]),
        )

    count, steps = len(stages), planes - 1
    order = [m for k in range(1, planes // 2) for m in (planes - k, k)] + [planes // 2, 0]
    around = [planes // 2], [d for d in range(1, planes) if d != planes // 2]
    live = {f"pieces{stage}": to_trade(stage) for stage in range(count)}
    own, normed, rows_of, sums = {}, {}, {}, {}

    chains = {}

    def split(stage, halves_of_terms):
        terms = [half[m] for half in halves_of_terms for m in range(planes // 2)]
        parts = CHAINS[stage]
        rows = stages[stage][1] // parts
        chains[stage] = [
            [terms[order.index(m)][part * rows : (part + 1) * rows] for m in range(planes)]
            for part in range(parts)
        ]
        sums[stage] = [None] * parts

    def next_sums(stage, step):
        sent = [
            onward(step, terms, arrived) for terms, arrived in zip(chains[stage], sums[stage])
        ]
        return [send_sums(step, *pair) for pair in sent]

    for now in range(ROUNDS[-1][-1]):
        fresh = {"weight": other_weight} if now == 0 else {}
        for stage, (to_shares, across, near, far, product, first) in enumerate(ROUNDS):
            if now < to_shares:
                fresh[f"pieces{stage}"] = live[f"pieces{stage}"]
            if now == to_shares:
                fresh[f"trade{stage}"] = trade(live[f"pieces{stage}"])
            if now == across[0]:
                normed[stage] = turned(normalize(live[f"trade{stage}"]))
                rows_of[stage] = {0: pick(normed[stage], column ^ plane)}
            for at, distances in zip(across, around):
                if now == at:
                    fresh[f"planes{stage}{distances[0]}"] = to_planes(normed[stage], distances)
            if now == near:
                own[stage] = jnp.stack([rows_of[stage][m] for m in order])
                fresh[f"near{stage}"] = spread_near(own[stage], columns)
            if now == far:
                fresh[f"near{stage}"] = live[f"near{stage}"]
                fresh[f"far{stage}"] = spread_far(live[f"near{stage}"], columns)
            if now == product:
                lefts = spread_all(own[stage], live[f"near{stage}"], live[f"far{stage}"])
                fresh[f"terms{stage}"] = [
                    partial_sums(place, lefts, half, 2, own_weight, other_weight)
                    for half in range(2)
                ]
                if now == first:
                    split(stage, fresh.pop(f"terms{stage}"))
            if first <= now < first + steps:
                fresh[f"sums{stage}"] = next_sums(stage, now - first + 1)
        live = together(fresh)
        other_weight = live.pop("weight", other_weight)
        for stage in range(count):
            for distances in around:
                rows_of.get(stage, {}).update(live.pop(f"planes{stage}{distances[0]}", {}))
            if f"sums{stage}" in live:
                sums[stage] = live.pop(f"sums{stage}")
            if f"terms{stage}" in live:
                split(stage, live.pop(f"terms{stage}"))
    for step in range(1, planes):
        sums[count - 1] = next_sums(count - 1, step)

    def summed(stage):
        parts = []
        for terms, (right, left) in zip(chains[stage], sums[stage]):
            total = terms[0].astype(jnp.float32)
            total = total + right.astype(jnp.float32) + left.astype(jnp.float32)
            parts.append(total.astype(jnp.bfloat16))
        return parts

    totals = {stage: summed(stage) for stage in range(count)}
    totals[0] = jnp.concatenate(totals[0], axis=0)
    rim, gated_rim = rims(totals[0], short_filter, long_count)
    projected = jnp.concatenate([*totals[1], totals[0]], axis=0)
    return finish(projected, rim, gated_rim, short_filter, long_filter)


def solution(mesh):
    return jax.shard_map(
        on_device,
        mesh=mesh,
        in_specs=(
            P("ctx", "fsdp"),
            P(),
            P("ctx", None, "fsdp"),
            P(None, None, "fsdp"),
            P(None, "fsdp"),
        ),
        out_specs=P("ctx", "fsdp"),
        check_vma=False,
    )
```

```python
import jax
import jax.numpy as jnp
import numpy as np
from jax import lax
from jax.experimental import pallas as pl
from jax.experimental.pallas import tpu as pltpu
from jax.sharding import PartitionSpec as P

CORES = 2
EPS = 1e-06
STAGES = (3, 5)
ROUNDS = ((0, (1, 1), 2, 3, 4, 4), (1, (2, 3), 4, 5, 6, 7))
CHAINS = (1, 2)
LANES = 128
RIM = 16


def pick(stack, index):
    return lax.dynamic_index_in_dim(stack, index, 0, keepdims=False)


def swap(value, count, bits):
    if bits == 0:
        return value
    return lax.ppermute(value, "fsdp", [(j, j ^ bits) for j in range(count)])


def plane_shift(value, edges):
    return lax.ppermute(
        value, "ctx", [(a * CORES + c, b * CORES + c) for a, b in edges for c in range(CORES)]
    )


def dft_matrices(length, taps):
    bins = length // 2 + 1
    room = -(-bins // 8) * 8
    k = np.arange(bins)[:, None]
    angle = 2.0 * np.pi * ((k * np.arange(length)[None, :]) % length) / length
    weight = np.where((k == 0) | (k == length // 2), 1.0, 2.0) / length
    analysis = np.zeros((2, room, length))
    synthesis = np.zeros((2, room, length))
    analysis[:, :bins] = np.stack([np.cos(angle), -np.sin(angle)])
    synthesis[:, :bins] = np.stack([weight * np.cos(angle), -weight * np.sin(angle)])
    return (
        analysis.reshape(2 * room, length).astype(np.float32),
        synthesis.reshape(2 * room, length)[:, taps:].T.astype(np.float32),
    )


def tile(*extents):
    return 2 * LANES if all(e % (2 * LANES) == 0 for e in extents) else LANES


def halves(value):
    high = value.astype(jnp.bfloat16)
    return high, (value - high.astype(jnp.float32)).astype(jnp.bfloat16)


def dot(a, b):
    return jnp.dot(a, b, preferred_element_type=jnp.float32)


def finish_kernel(
    query, key, value, rims, short, long,
    analysis_high, analysis_low, synthesis_high, synthesis_low, out, extended, signal,
):
    row_count = out.shape[0]
    taps = long.shape[0]
    room = analysis_high.shape[0] // 2
    reach = short.shape[0]
    for b, body in enumerate((query, key, value)):
        extended[b, :8] = rims[taps + RIM * b : taps + RIM * (b + 1)].astype(jnp.float32)[RIM - 8 :]
        extended[b, 8:] = body[...].astype(jnp.float32)

    def featurized(b, start, count):
        result = None
        for s in range(reach):
            term = short[s, b : b + 1, :] * extended[b, 8 + start - s : 8 + start - s + count]
            result = term if result is None else result + term
        return result

    signal[:taps] = rims[:taps]
    for start in range(0, row_count, taps):
        gated = featurized(1, start, taps) * featurized(2, start, taps)
        signal[taps + start : 2 * taps + start] = gated.astype(jnp.bfloat16)

    long_high, long_low = halves(long[...])
    tones = (
        dot(analysis_high[:, :taps], long_high)
        + dot(analysis_high[:, :taps], long_low)
        + dot(analysis_low[:, :taps], long_high)
    )
    for start in range(0, row_count, taps):
        block = signal[start : start + 2 * taps]
        spectrum = dot(analysis_high[...], block) + dot(analysis_low[...], block)
        real = spectrum[:room] * tones[:room] - spectrum[room:] * tones[room:]
        imag = spectrum[:room] * tones[room:] + spectrum[room:] * tones[:room]
        high, low = halves(jnp.concatenate([real, imag], axis=0))
        response = (
            dot(synthesis_high[...], high)
            + dot(synthesis_high[...], low)
            + dot(synthesis_low[...], high)
        )
        out[start : start + taps] = (featurized(0, start, taps) * response).astype(out.dtype)


def finish(projected, rims, short_filter, long_filter):
    row_count = projected.shape[0]
    taps, channels = long_filter.shape
    width = tile(channels)
    count = channels // width
    analysis, synthesis = (jnp.asarray(m) for m in dft_matrices(2 * taps, taps))
    constants = (*halves(analysis), *halves(synthesis))

    def branch(b):
        return pl.BlockSpec((row_count, width), lambda i: (0, b * count + i))

    operands = [*[projected] * 3, rims, short_filter, long_filter, *constants]
    specs = (
        [branch(b) for b in range(3)]
        + [
            pl.BlockSpec((rims.shape[0], width), lambda i: (0, i)),
            pl.BlockSpec((short_filter.shape[0], 3, width), lambda i: (0, 0, i)),
            pl.BlockSpec((taps, width), lambda i: (0, i)),
        ]
        + [pl.BlockSpec(m.shape, lambda i: (0, 0)) for m in constants]
    )
    return pl.pallas_call(
        finish_kernel,
        out_shape=jax.ShapeDtypeStruct((row_count, channels), jnp.bfloat16),
        grid=(count,),
        in_specs=specs,
        out_specs=pl.BlockSpec((row_count, width), lambda i: (0, i)),
        scratch_shapes=[
            pltpu.VMEM((3, 8 + row_count, width), jnp.float32),
            pltpu.VMEM((taps + row_count, width), jnp.bfloat16),
        ],
        compiler_params=pltpu.CompilerParams(vmem_limit_bytes=32 * 1024 * 1024),
        cost_estimate=pl.CostEstimate(
            flops=row_count * channels * 5000, bytes_accessed=row_count * channels * 10, transcendentals=0
        ),
    )(*operands)


def passed_rims(last_rows, short_filter, long_count):
    reach = short_filter.shape[0]
    channels = short_filter.shape[2]
    total = last_rows.shape[0]
    branches = [last_rows[:, b * channels : (b + 1) * channels] for b in range(3)]
    mixed = []
    for b in (1, 2):
        rows = branches[b].astype(jnp.float32)
        mixed.append(
            sum(
                short_filter[s, b] * rows[total - long_count - s : total - s] for s in range(reach)
            )
        )
    gated = (mixed[0] * mixed[1]).astype(jnp.bfloat16)
    packed = jnp.concatenate([gated] + [rows[total - RIM :] for rows in branches], axis=0)
    count = lax.axis_size("ctx")
    return lax.ppermute(packed, "ctx", [(i, i + 1) for i in range(count - 1)])


def together(values):
    leaves, tree = jax.tree.flatten(values)
    anywhere = pl.BlockSpec(memory_space=pl.ANY)
    leaves = pl.pallas_call(
        lambda *refs: None,
        out_shape=[jax.ShapeDtypeStruct(leaf.shape, leaf.dtype) for leaf in leaves],
        in_specs=[anywhere] * len(leaves),
        out_specs=[anywhere] * len(leaves),
        input_output_aliases={at: at for at in range(len(leaves))},
    )(*leaves)
    return jax.tree.unflatten(tree, leaves)


def spread_near(value, columns):
    if columns != 4:
        return [swap(value, columns, t) for t in range(1, columns)]
    return [swap(value, columns, 1), swap(value, columns, 2)]


def spread_far(near, columns):
    if columns != 4:
        return []
    half = near[0].shape[-1] // 2
    return [swap(near[1][..., :half], columns, 1), swap(near[0][..., half:], columns, 2)]


def spread_all(value, near, far):
    return [value, *near] + ([jnp.concatenate(far, axis=-1)] if far else [])


def partial_kernel(place, *refs):
    *lefts, own, other, out, joined = refs
    planes, columns, share, depth = joined.shape

    @pl.when(pl.program_id(0) == 0)
    def _():
        for t, left in enumerate(lefts):
            joined[:, place[0] ^ t] = left[...]

    rows = joined[...].reshape(planes * columns * share, depth)
    half = depth // 2
    total = dot(rows[:, :half], own[0]) + dot(rows[:, half:], other[0])
    out[...] = total.astype(out.dtype)


def partial_sums(place, lefts, own, other, size, at):
    _, share, depth = lefts[0].shape
    columns = len(lefts)
    channels = own.shape[2]
    rows = size * columns * share
    weights = pl.BlockSpec((1, own.shape[1], channels), lambda b, _: (b, 0, 0))
    left = pl.BlockSpec(
        (size, share, depth), lambda b, place: (place[1] if at is None else at, 0, 0)
    )
    return pl.pallas_call(
        partial_kernel,
        out_shape=jax.ShapeDtypeStruct((rows, 3 * channels), jnp.bfloat16),
        grid_spec=pltpu.PrefetchScalarGridSpec(
            num_scalar_prefetch=1,
            grid=(3,),
            in_specs=[left] * columns + [weights, weights],
            out_specs=pl.BlockSpec((rows, channels), lambda b, _: (0, b)),
            scratch_shapes=[pltpu.VMEM((size, columns, share, depth), jnp.bfloat16)],
        ),
        compiler_params=pltpu.CompilerParams(vmem_limit_bytes=56 * 1024 * 1024),
        cost_estimate=pl.CostEstimate(
            flops=2 * rows * depth * 3 * channels,
            bytes_accessed=2 * rows * depth + 6 * depth * channels + 6 * rows * channels,
            transcendentals=0,
        ),
    )(place, *lefts, own, other).reshape(size, columns * share, 3 * channels)


def on_device(tokens, gain, in_weight, short_filter, long_filter):
    planes = lax.axis_size("ctx") // CORES
    columns = lax.axis_size("fsdp")
    plane = lax.axis_index("ctx") // CORES
    core = lax.axis_index("ctx") % CORES
    column = lax.axis_index("fsdp")
    early_half = plane < planes // 2
    place = jnp.stack([column, jnp.where(early_half, 0, 1)]).astype(jnp.int32)
    row_count, width = tokens.shape
    long_count = long_filter.shape[0]

    parts = STAGES
    if row_count % (sum(parts) * columns * RIM):
        parts = (1, 1)
    unit = row_count // sum(parts)
    sizes = [unit * part for part in parts]
    stages = [(row_count - sizes[0], sizes[0]), (0, sizes[1])]

    weight = jnp.transpose(in_weight, (1, 0, 2))
    other_weight = lax.ppermute(
        weight,
        "ctx",
        [(p * CORES + c, p * CORES + 1 - c) for p in range(planes) for c in range(CORES)],
    )

    gains = gain.reshape(columns, width)
    gain_here = jnp.stack([pick(gains, column ^ t) for t in range(columns)])[:, None, :]

    def to_trade(stage):
        start, size = stages[stage]
        rows = tokens[start : start + size].reshape(columns, -1, width)
        return [pick(rows, column ^ t) for t in range(columns)]

    def trade(pieces):
        return [swap(piece, columns, t) for t, piece in enumerate(pieces)]

    def normalize(wide):
        wide = jnp.stack(wide).astype(jnp.float32)
        mean_square = jnp.sum(wide * wide, axis=(0, 2), keepdims=True) / (columns * width)
        normed = (wide * lax.rsqrt(mean_square + EPS) * gain_here).astype(jnp.bfloat16)
        return jnp.where(core == 0, normed, jnp.roll(normed, width // 2, axis=2))

    def to_planes(normed, distances):
        rows_of = {}
        for d in distances:
            piece = pick(normed, column ^ ((plane + d) % planes))
            rows_of[planes - d] = plane_shift(piece, [(p, (p + d) % planes) for p in range(planes)])
        return rows_of

    def send_sums(step, terms, arrived, sent=None):
        def onward(term, came):
            if came is None:
                return term
            return (term.astype(jnp.float32) + came.astype(jnp.float32)).astype(jnp.bfloat16)

        right = [(p, p + 1) for p in range(planes - 1) if p < step]
        left = [(p, p - 1) for p in range(1, planes) if p >= planes - step]
        if 2 * step < planes:
            if sent is None:
                sent = jnp.where(early_half, terms[planes - step], terms[step])
            return [plane_shift(onward(sent, arrived[0]), right + left)]
        return [
            plane_shift(onward(terms[planes - step], arrived[0]), right),
            plane_shift(onward(terms[step], arrived[-1]), left),
        ]

    count, steps = len(stages), planes - 1
    order = [m for k in range(1, planes // 2) for m in (planes - k, k)] + [planes // 2, 0]
    around = [planes // 2], [d for d in range(1, planes) if d != planes // 2]
    chains, sums = {}, {}
    normed, rows_of, own, lefts = {}, {}, {}, {}

    def product(stage, size, at):
        return partial_sums(place, lefts[stage], weight, other_weight, size, at)

    def split(stage, blocks):
        terms = [block for part in blocks for block in part]
        rows = stages[stage][1] // CHAINS[stage]
        chains[stage] = [
            [terms[order.index(m)][part * rows : (part + 1) * rows] for m in range(planes)]
            for part in range(CHAINS[stage])
        ]
        sums[stage] = [[None]] * CHAINS[stage]

    live = {f"pieces{stage}": to_trade(stage) for stage in range(count)}
    for now in range(ROUNDS[-1][-1]):
        fresh = {"weight": other_weight} if now == 0 else {}
        for stage, (to_shares, across, near, far, ready, first) in enumerate(ROUNDS):
            if now < to_shares:
                fresh[f"pieces{stage}"] = live[f"pieces{stage}"]
            if now == to_shares:
                fresh[f"trade{stage}"] = trade(live[f"pieces{stage}"])
            if now == across[0]:
                normed[stage] = normalize(live[f"trade{stage}"])
                rows_of[stage] = {0: pick(normed[stage], column ^ plane)}
            for at, distances in zip(across, around):
                if now == at:
                    fresh[f"planes{stage}{distances[0]}"] = to_planes(normed[stage], distances)
            if now == near:
                own[stage] = jnp.stack([rows_of[stage][m] for m in order])
                fresh[f"near{stage}"] = spread_near(own[stage], columns)
            if now == far:
                fresh[f"near{stage}"] = live[f"near{stage}"]
                fresh[f"far{stage}"] = spread_far(live[f"near{stage}"], columns)
            if now == ready:
                lefts[stage] = spread_all(own[stage], live[f"near{stage}"], live[f"far{stage}"])
                if now == first:
                    lead = product(stage, 1, None)[0]
                    split(stage, [product(stage, planes, 0)])
                    fresh[f"sums{stage}"] = [send_sums(1, chains[stage][0], [None], lead)]
                else:
                    fresh[f"lead{stage}"] = product(stage, planes // 2, 0)
            if first < now < first + steps:
                fresh[f"sums{stage}"] = [
                    send_sums(now - first + 1, terms, arrived)
                    for terms, arrived in zip(chains[stage], sums[stage])
                ]
        live = together(fresh)
        other_weight = live.pop("weight", other_weight)
        for stage in range(count):
            for distances in around:
                rows_of.get(stage, {}).update(live.pop(f"planes{stage}{distances[0]}", {}))
            if f"sums{stage}" in live:
                sums[stage] = live.pop(f"sums{stage}")

    last = count - 1
    split(last, [live[f"lead{last}"], product(last, planes // 2, 1)])
    for step in range(1, planes):
        sums[last] = [
            send_sums(step, terms, arrived) for terms, arrived in zip(chains[last], sums[last])
        ]

    def summed(stage):
        parts = []
        for terms, arrived in zip(chains[stage], sums[stage]):
            total = terms[0].astype(jnp.float32)
            total = total + arrived[0].astype(jnp.float32) + arrived[-1].astype(jnp.float32)
            parts.append(total.astype(jnp.bfloat16))
        return parts

    (last_rows,) = summed(0)
    rims = passed_rims(last_rows, short_filter, long_count)
    projected = jnp.concatenate([*summed(1), last_rows], axis=0)
    return finish(projected, rims, short_filter, long_filter)


def solution(mesh):
    return jax.shard_map(
        on_device,
        mesh=mesh,
        in_specs=(
            P("ctx", "fsdp"),
            P(),
            P("ctx", None, "fsdp"),
            P(None, None, "fsdp"),
            P(None, "fsdp"),
        ),
        out_specs=P("ctx", "fsdp"),
        check_vma=False,
    )
```

```python
import jax
import jax.numpy as jnp
import numpy as np
from jax import lax
from jax.experimental import pallas as pl
from jax.experimental.pallas import tpu as pltpu
from jax.sharding import PartitionSpec as P

CORES = 2
EPS = 1e-06
STAGES = (3, 5)
ROUNDS = ((0, (1, 1), 2, 3, 4, 4), (1, (2, 3), 4, 5, 6, 7))
CHAINS = (1, 2)
RIM = 16


def pick(stack, index):
    return lax.dynamic_index_in_dim(stack, index, 0, keepdims=False)


def swap(value, count, bits):
    if bits == 0:
        return value
    return lax.ppermute(value, "fsdp", [(j, j ^ bits) for j in range(count)])


def plane_shift(value, edges):
    return lax.ppermute(
        value, "ctx", [(a * CORES + c, b * CORES + c) for a, b in edges for c in range(CORES)]
    )


def dft_matrices(length):
    half = length // 2
    k = np.concatenate([np.arange(half), [half], np.arange(1, half)])[:, None]
    angle = 2.0 * np.pi * ((k * np.arange(length)[None, :]) % length) / length
    wave = np.where(np.arange(length)[:, None] <= half, np.cos(angle), -np.sin(angle))
    weight = np.where((k == 0) | (k == half), 1.0, 2.0) / length
    return wave.astype(np.float32), (weight * wave)[:, half:].T.astype(np.float32)


def halves(value):
    high = value.astype(jnp.bfloat16)
    return high, (value - high.astype(jnp.float32)).astype(jnp.bfloat16)


def dot(a, b):
    return jnp.dot(a, b, preferred_element_type=jnp.float32)


def finish_kernel(
    query, key, value, rims, short, long, analysis, synthesis, out, extended, signal
):
    row_count = out.shape[0]
    taps = long.shape[0]
    length = 2 * taps
    reach = short.shape[0]
    for b, body in enumerate((query, key, value)):
        extended[b, :8] = rims[taps + RIM * b : taps + RIM * (b + 1)].astype(jnp.float32)[RIM - 8 :]
        extended[b, 8:] = body[...].astype(jnp.float32)

    def featurized(b, start, count):
        result = None
        for s in range(reach):
            term = short[s, b : b + 1, :] * extended[b, 8 + start - s : 8 + start - s + count]
            result = term if result is None else result + term
        return result

    signal[:taps] = rims[:taps]
    for start in range(0, row_count, taps):
        gated = featurized(1, start, taps) * featurized(2, start, taps)
        signal[taps + start : 2 * taps + start] = gated.astype(jnp.bfloat16)

    def both(product):
        return product[: product.shape[0] // 2] + product[product.shape[0] // 2 :]

    long_high, long_low = halves(long[...])
    tones = both(dot(analysis[:, :taps], long_high)) + dot(analysis[:length, :taps], long_low)
    first = lax.broadcasted_iota(jnp.int32, (taps, tones.shape[1]), 0) == 0
    real_tones = tones[:taps]
    cross_tones = jnp.where(first, 0.0, tones[taps:])
    last_tones = jnp.where(first, tones[taps:], tones[:taps])
    for start in range(0, row_count, taps):
        spectrum = both(dot(analysis[...], signal[start : start + length]))
        real, imag = spectrum[:taps], spectrum[taps:]
        high, low = halves(
            jnp.concatenate(
                [
                    real * real_tones - imag * cross_tones,
                    real * cross_tones + imag * last_tones,
                ],
                axis=0,
            )
        )
        response = both(dot(synthesis[...], high)) + dot(synthesis[:taps], low)
        out[start : start + taps] = (featurized(0, start, taps) * response).astype(out.dtype)


def finish(projected, rims, short_filter, long_filter):
    row_count = projected.shape[0]
    taps, channels = long_filter.shape
    constants = [
        jnp.concatenate(halves(jnp.asarray(matrix)), axis=0) for matrix in dft_matrices(2 * taps)
    ]

    def branch(b):
        return pl.BlockSpec((row_count, channels), lambda i: (0, b))

    operands = [*[projected] * 3, rims, short_filter, long_filter, *constants]
    specs = (
        [branch(b) for b in range(3)]
        + [
            pl.BlockSpec(rims.shape, lambda i: (0, 0)),
            pl.BlockSpec(short_filter.shape, lambda i: (0, 0, 0)),
            pl.BlockSpec(long_filter.shape, lambda i: (0, 0)),
        ]
        + [pl.BlockSpec(m.shape, lambda i: (0, 0)) for m in constants]
    )
    return pl.pallas_call(
        finish_kernel,
        out_shape=jax.ShapeDtypeStruct((row_count, channels), jnp.bfloat16),
        grid=(1,),
        in_specs=specs,
        out_specs=pl.BlockSpec((row_count, channels), lambda i: (0, 0)),
        scratch_shapes=[
            pltpu.VMEM((3, 8 + row_count, channels), jnp.float32),
            pltpu.VMEM((taps + row_count, channels), jnp.bfloat16),
        ],
        compiler_params=pltpu.CompilerParams(vmem_limit_bytes=32 * 1024 * 1024),
        cost_estimate=pl.CostEstimate(
            flops=row_count * channels * 5000, bytes_accessed=row_count * channels * 10, transcendentals=0
        ),
    )(*operands)


def passed_rims(last_rows, short_filter, long_count):
    reach = short_filter.shape[0]
    channels = short_filter.shape[2]
    total = last_rows.shape[0]
    branches = [last_rows[:, b * channels : (b + 1) * channels] for b in range(3)]
    mixed = []
    for b in (1, 2):
        rows = branches[b].astype(jnp.float32)
        mixed.append(
            sum(
                short_filter[s, b] * rows[total - long_count - s : total - s] for s in range(reach)
            )
        )
    gated = (mixed[0] * mixed[1]).astype(jnp.bfloat16)
    packed = jnp.concatenate([gated] + [rows[total - RIM :] for rows in branches], axis=0)
    count = lax.axis_size("ctx")
    return lax.ppermute(packed, "ctx", [(i, i + 1) for i in range(count - 1)])


def together(values):
    leaves, tree = jax.tree.flatten(values)
    anywhere = pl.BlockSpec(memory_space=pl.ANY)
    leaves = pl.pallas_call(
        lambda *refs: None,
        out_shape=[jax.ShapeDtypeStruct(leaf.shape, leaf.dtype) for leaf in leaves],
        in_specs=[anywhere] * len(leaves),
        out_specs=[anywhere] * len(leaves),
        input_output_aliases={at: at for at in range(len(leaves))},
    )(*leaves)
    return jax.tree.unflatten(tree, leaves)


def spread_near(value, columns):
    if columns != 4:
        return [swap(value, columns, t) for t in range(1, columns)]
    return [swap(value, columns, 1), swap(value, columns, 2)]


def spread_far(near, columns):
    if columns != 4:
        return []
    half = near[0].shape[0] // 2
    return [swap(near[1][:half], columns, 1), swap(near[0][half:], columns, 2)]


def partial_kernel(parts, place, *refs):
    *lefts, own, other, out, joined = refs
    size, columns, share, depth = joined.shape

    @pl.when((pl.program_id(0) == 0) & (pl.program_id(1) == 0))
    def _():
        for (t, begin, end), left in zip(parts, lefts):
            joined[begin:end, place[0] ^ t] = left[...]

    rows = joined[...].reshape(size * columns * share, depth)
    half = depth // 2
    total = dot(rows[:, :half], own[0]) + dot(rows[:, half:], other[0])
    out[...] = total.astype(out.dtype)


def partial_sums(place, lefts, far, own, other, size, at):
    planes, share, depth = lefts[0].shape
    columns = len(lefts) + (1 if far else 0)
    channels = own.shape[2]
    rows = size * columns * share
    width = channels
    count = channels // width
    weights = pl.BlockSpec((1, own.shape[1], width), lambda b, n, _: (b, 0, n))

    def block(shape, before=0):
        return pl.BlockSpec(
            shape, lambda b, n, place: (place[1] if at is None else at - before, 0, 0)
        )

    operands = list(lefts)
    specs = [block((size, share, depth)) for _ in lefts]
    parts = [(t, 0, size) for t in range(len(lefts))]
    if far and size == planes:
        operands += far
        specs += [pl.BlockSpec(part.shape, lambda b, n, _: (0, 0, 0)) for part in far]
        parts += [(len(lefts), 0, planes // 2), (len(lefts), planes // 2, planes)]
    elif far:
        second = at is not None and at * size >= planes // 2
        operands.append(far[second])
        specs.append(block((size, share, depth), planes // 2 // size if second else 0))
        parts.append((len(lefts), 0, size))
    return pl.pallas_call(
        lambda *refs: partial_kernel(parts, *refs),
        out_shape=jax.ShapeDtypeStruct((rows, 3 * channels), jnp.bfloat16),
        grid_spec=pltpu.PrefetchScalarGridSpec(
            num_scalar_prefetch=1,
            grid=(3, count),
            in_specs=specs + [weights, weights],
            out_specs=pl.BlockSpec((rows, width), lambda b, n, _: (0, b * count + n)),
            scratch_shapes=[pltpu.VMEM((size, columns, share, depth), jnp.bfloat16)],
        ),
        compiler_params=pltpu.CompilerParams(
            vmem_limit_bytes=(56 if size == 1 else 36) * 1024 * 1024
        ),
        cost_estimate=pl.CostEstimate(
            flops=2 * rows * depth * 3 * channels,
            bytes_accessed=2 * rows * depth + 6 * depth * channels + 6 * rows * channels,
            transcendentals=0,
        ),
    )(place, *operands, own, other).reshape(size, columns * share, 3 * channels)


def on_device(tokens, gain, in_weight, short_filter, long_filter):
    planes = lax.axis_size("ctx") // CORES
    columns = lax.axis_size("fsdp")
    plane = lax.axis_index("ctx") // CORES
    core = lax.axis_index("ctx") % CORES
    column = lax.axis_index("fsdp")
    early_half = plane < planes // 2
    place = jnp.stack([column, jnp.where(early_half, 0, 1)]).astype(jnp.int32)
    row_count, width = tokens.shape
    long_count = long_filter.shape[0]

    parts = STAGES
    if row_count % (sum(parts) * columns * RIM):
        parts = (1, 1)
    unit = row_count // sum(parts)
    sizes = [unit * part for part in parts]
    stages = [(row_count - sizes[0], sizes[0]), (0, sizes[1])]

    weight = jnp.transpose(in_weight, (1, 0, 2))
    other_weight = lax.ppermute(
        weight,
        "ctx",
        [(p * CORES + c, p * CORES + 1 - c) for p in range(planes) for c in range(CORES)],
    )

    gains = gain.reshape(columns, width)
    gain_here = jnp.stack([pick(gains, column ^ t) for t in range(columns)])[:, None, :]

    def to_trade(stage):
        start, size = stages[stage]
        rows = tokens[start : start + size].reshape(columns, -1, width)
        return [pick(rows, column ^ t) for t in range(columns)]

    def trade(pieces):
        return [swap(piece, columns, t) for t, piece in enumerate(pieces)]

    def normalize(wide):
        wide = jnp.stack(wide).astype(jnp.float32)
        mean_square = jnp.sum(wide * wide, axis=(0, 2), keepdims=True) / (columns * width)
        normed = (wide * lax.rsqrt(mean_square + EPS) * gain_here).astype(jnp.bfloat16)
        return jnp.where(core == 0, normed, jnp.roll(normed, width // 2, axis=2))

    def to_planes(normed, distances):
        rows_of = {}
        for d in distances:
            piece = pick(normed, column ^ ((plane + d) % planes))
            rows_of[planes - d] = plane_shift(piece, [(p, (p + d) % planes) for p in range(planes)])
        return rows_of

    def send_sums(step, terms, arrived, sent=None):
        def onward(term, came):
            if came is None:
                return term
            return (term.astype(jnp.float32) + came.astype(jnp.float32)).astype(jnp.bfloat16)

        right = [(p, p + 1) for p in range(planes - 1) if p < step]
        left = [(p, p - 1) for p in range(1, planes) if p >= planes - step]
        if 2 * step < planes:
            if sent is None:
                sent = jnp.where(early_half, terms[planes - step], terms[step])
            return [plane_shift(onward(sent, arrived[0]), right + left)]
        return [
            plane_shift(onward(terms[planes - step], arrived[0]), right),
            plane_shift(onward(terms[step], arrived[-1]), left),
        ]

    count, steps = len(stages), planes - 1
    order = [m for k in range(1, planes // 2) for m in (planes - k, k)] + [planes // 2, 0]
    around = [planes // 2], [d for d in range(1, planes) if d != planes // 2]
    chains, sums = {}, {}
    normed, rows_of, own, lefts = {}, {}, {}, {}

    def product(stage, size, at):
        return partial_sums(place, *lefts[stage], weight, other_weight, size, at)

    def split(stage, blocks):
        terms = [block for part in blocks for block in part]
        rows = stages[stage][1] // CHAINS[stage]
        chains[stage] = [
            [terms[order.index(m)][part * rows : (part + 1) * rows] for m in range(planes)]
            for part in range(CHAINS[stage])
        ]
        sums[stage] = [[None]] * CHAINS[stage]

    live = {f"pieces{stage}": to_trade(stage) for stage in range(count)}
    for now in range(ROUNDS[-1][-1]):
        fresh = {"weight": other_weight} if now == 0 else {}
        for stage, (to_shares, across, near, far, ready, first) in enumerate(ROUNDS):
            if now < to_shares:
                fresh[f"pieces{stage}"] = live[f"pieces{stage}"]
            if now == to_shares:
                fresh[f"trade{stage}"] = trade(live[f"pieces{stage}"])
            if now == across[0]:
                normed[stage] = normalize(live[f"trade{stage}"])
                rows_of[stage] = {0: pick(normed[stage], column ^ plane)}
            for at, distances in zip(across, around):
                if now == at:
                    fresh[f"planes{stage}{distances[0]}"] = to_planes(normed[stage], distances)
            if now == near:
                own[stage] = jnp.stack([rows_of[stage][m] for m in order])
                fresh[f"near{stage}"] = spread_near(own[stage], columns)
            if now == far:
                fresh[f"near{stage}"] = live[f"near{stage}"]
                fresh[f"far{stage}"] = spread_far(live[f"near{stage}"], columns)
            if now == ready:
                lefts[stage] = [own[stage], *live[f"near{stage}"]], live[f"far{stage}"]
                if now == first:
                    lead = product(stage, 1, None)[0]
                    split(stage, [product(stage, planes, 0)])
                    fresh[f"sums{stage}"] = [send_sums(1, chains[stage][0], [None], lead)]
                else:
                    fresh[f"lead{stage}"] = product(stage, planes // 2, 0)
            if first < now < first + steps:
                fresh[f"sums{stage}"] = [
                    send_sums(now - first + 1, terms, arrived)
                    for terms, arrived in zip(chains[stage], sums[stage])
                ]
        live = together(fresh)
        other_weight = live.pop("weight", other_weight)
        for stage in range(count):
            for distances in around:
                rows_of.get(stage, {}).update(live.pop(f"planes{stage}{distances[0]}", {}))
            if f"sums{stage}" in live:
                sums[stage] = live.pop(f"sums{stage}")

    last = count - 1
    split(last, [live[f"lead{last}"], product(last, planes // 2, 1)])
    for step in range(1, planes):
        sums[last] = [
            send_sums(step, terms, arrived) for terms, arrived in zip(chains[last], sums[last])
        ]

    def summed(stage):
        parts = []
        for terms, arrived in zip(chains[stage], sums[stage]):
            total = terms[0].astype(jnp.float32)
            total = total + arrived[0].astype(jnp.float32) + arrived[-1].astype(jnp.float32)
            parts.append(total.astype(jnp.bfloat16))
        return parts

    (last_rows,) = summed(0)
    rims = passed_rims(last_rows, short_filter, long_count)
    projected = jnp.concatenate([*summed(1), last_rows], axis=0)
    return finish(projected, rims, short_filter, long_filter)


def solution(mesh):
    return jax.shard_map(
        on_device,
        mesh=mesh,
        in_specs=(
            P("ctx", "fsdp"),
            P(),
            P("ctx", None, "fsdp"),
            P(None, None, "fsdp"),
            P(None, "fsdp"),
        ),
        out_specs=P("ctx", "fsdp"),
        check_vma=False,
    )
```

```python
import jax
import jax.numpy as jnp
import numpy as np
from jax import lax
from jax.experimental import pallas as pl
from jax.experimental.pallas import tpu as pltpu
from jax.sharding import PartitionSpec as P

CORES = 2
EPS = 1e-06
STAGES = (3, 5)
ROUNDS = ((0, (1, 1), 2, 3, 4, 4), (1, (2, 3), 4, 5, 6, 7))
LOOSE = (("planes12", 2), ("near1", 4), ("sums0", 4))
CHAINS = (1, 2)
RIM = 16


def pick(stack, index):
    return lax.dynamic_index_in_dim(stack, index, 0, keepdims=False)


def swap(value, count, bits):
    if bits == 0:
        return value
    return lax.ppermute(value, "fsdp", [(j, j ^ bits) for j in range(count)])


def plane_shift(value, edges):
    return lax.ppermute(
        value, "ctx", [(a * CORES + c, b * CORES + c) for a, b in edges for c in range(CORES)]
    )


def dft_matrices(length):
    half = length // 2
    k = np.concatenate([np.arange(half), [half], np.arange(1, half)])[:, None]
    angle = 2.0 * np.pi * ((k * np.arange(length)[None, :]) % length) / length
    wave = np.where(np.arange(length)[:, None] <= half, np.cos(angle), -np.sin(angle))
    weight = np.where((k == 0) | (k == half), 1.0, 2.0) / length
    return wave.astype(np.float32), (weight * wave)[:, half:].T.astype(np.float32)


def halves(value):
    high = value.astype(jnp.bfloat16)
    return high, (value - high.astype(jnp.float32)).astype(jnp.bfloat16)


def dot(a, b):
    return jnp.dot(a, b, preferred_element_type=jnp.float32)


def finish_kernel(
    query, key, value, rims, short, long, analysis, synthesis, out, extended, signal
):
    row_count = out.shape[0]
    taps = long.shape[0]
    length = 2 * taps
    reach = short.shape[0]
    for b, body in enumerate((query, key, value)):
        extended[b, :8] = rims[taps + RIM * b : taps + RIM * (b + 1)].astype(jnp.float32)[RIM - 8 :]
        extended[b, 8:] = body[...].astype(jnp.float32)

    def featurized(b, start, count):
        result = None
        for s in range(reach):
            term = short[s, b : b + 1, :] * extended[b, 8 + start - s : 8 + start - s + count]
            result = term if result is None else result + term
        return result

    signal[:taps] = rims[:taps]
    for start in range(0, row_count, taps):
        gated = featurized(1, start, taps) * featurized(2, start, taps)
        signal[taps + start : 2 * taps + start] = gated.astype(jnp.bfloat16)

    def both(product):
        return product[: product.shape[0] // 2] + product[product.shape[0] // 2 :]

    long_high, long_low = halves(long[...])
    tones = both(dot(analysis[:, :taps], long_high)) + dot(analysis[:length, :taps], long_low)
    first = lax.broadcasted_iota(jnp.int32, (taps, tones.shape[1]), 0) == 0
    real_tones = tones[:taps]
    cross_tones = jnp.where(first, 0.0, tones[taps:])
    last_tones = jnp.where(first, tones[taps:], tones[:taps])
    for start in range(0, row_count, taps):
        spectrum = both(dot(analysis[...], signal[start : start + length]))
        real, imag = spectrum[:taps], spectrum[taps:]
        high, low = halves(
            jnp.concatenate(
                [
                    real * real_tones - imag * cross_tones,
                    real * cross_tones + imag * last_tones,
                ],
                axis=0,
            )
        )
        response = both(dot(synthesis[...], high)) + dot(synthesis[:taps], low)
        out[start : start + taps] = (featurized(0, start, taps) * response).astype(out.dtype)


def finish(projected, rims, short_filter, long_filter):
    row_count = projected.shape[0]
    taps, channels = long_filter.shape
    constants = [
        jnp.concatenate(halves(jnp.asarray(matrix)), axis=0) for matrix in dft_matrices(2 * taps)
    ]

    def branch(b):
        return pl.BlockSpec((row_count, channels), lambda i: (0, b))

    operands = [*[projected] * 3, rims, short_filter, long_filter, *constants]
    specs = (
        [branch(b) for b in range(3)]
        + [
            pl.BlockSpec(rims.shape, lambda i: (0, 0)),
            pl.BlockSpec(short_filter.shape, lambda i: (0, 0, 0)),
            pl.BlockSpec(long_filter.shape, lambda i: (0, 0)),
        ]
        + [pl.BlockSpec(m.shape, lambda i: (0, 0)) for m in constants]
    )
    return pl.pallas_call(
        finish_kernel,
        out_shape=jax.ShapeDtypeStruct((row_count, channels), jnp.bfloat16),
        grid=(1,),
        in_specs=specs,
        out_specs=pl.BlockSpec((row_count, channels), lambda i: (0, 0)),
        scratch_shapes=[
            pltpu.VMEM((3, 8 + row_count, channels), jnp.float32),
            pltpu.VMEM((taps + row_count, channels), jnp.bfloat16),
        ],
        compiler_params=pltpu.CompilerParams(vmem_limit_bytes=32 * 1024 * 1024),
        cost_estimate=pl.CostEstimate(
            flops=row_count * channels * 5000, bytes_accessed=row_count * channels * 10, transcendentals=0
        ),
    )(*operands)


def passed_rims(last_rows, short_filter, long_count):
    reach = short_filter.shape[0]
    channels = short_filter.shape[2]
    total = last_rows.shape[0]
    branches = [last_rows[:, b * channels : (b + 1) * channels] for b in range(3)]
    mixed = []
    for b in (1, 2):
        rows = branches[b].astype(jnp.float32)
        mixed.append(
            sum(
                short_filter[s, b] * rows[total - long_count - s : total - s] for s in range(reach)
            )
        )
    gated = (mixed[0] * mixed[1]).astype(jnp.bfloat16)
    packed = jnp.concatenate([gated] + [rows[total - RIM :] for rows in branches], axis=0)
    count = lax.axis_size("ctx")
    return lax.ppermute(packed, "ctx", [(i, i + 1) for i in range(count - 1)])


def together(values):
    leaves, tree = jax.tree.flatten(values)
    anywhere = pl.BlockSpec(memory_space=pl.ANY)
    leaves = pl.pallas_call(
        lambda *refs: None,
        out_shape=[jax.ShapeDtypeStruct(leaf.shape, leaf.dtype) for leaf in leaves],
        in_specs=[anywhere] * len(leaves),
        out_specs=[anywhere] * len(leaves),
        input_output_aliases={at: at for at in range(len(leaves))},
    )(*leaves)
    return jax.tree.unflatten(tree, leaves)


def spread_near(value, columns):
    if columns != 4:
        return [swap(value, columns, t) for t in range(1, columns)]
    return [swap(value, columns, 1), swap(value, columns, 2)]


def spread_far(near, columns):
    if columns != 4:
        return []
    half = near[0].shape[0] // 2
    return [swap(near[1][:half], columns, 1), swap(near[0][half:], columns, 2)]


def partial_kernel(parts, place, *refs):
    *lefts, own, other, out, joined = refs
    size, columns, share, depth = joined.shape

    @pl.when((pl.program_id(0) == 0) & (pl.program_id(1) == 0))
    def _():
        for (t, begin, end), left in zip(parts, lefts):
            joined[begin:end, place[0] ^ t] = left[...]

    rows = joined[...].reshape(size * columns * share, depth)
    half = depth // 2
    total = dot(rows[:, :half], own[0]) + dot(rows[:, half:], other[0])
    out[...] = total.astype(out.dtype)


def partial_sums(place, lefts, far, own, other, size, at):
    planes, share, depth = lefts[0].shape
    columns = len(lefts) + (1 if far else 0)
    channels = own.shape[2]
    rows = size * columns * share
    width = channels
    count = channels // width
    weights = pl.BlockSpec((1, own.shape[1], width), lambda b, n, _: (b, 0, n))

    def block(shape, before=0):
        return pl.BlockSpec(
            shape, lambda b, n, place: (place[1] if at is None else at - before, 0, 0)
        )

    operands = list(lefts)
    specs = [block((size, share, depth)) for _ in lefts]
    parts = [(t, 0, size) for t in range(len(lefts))]
    if far and size == planes:
        operands += far
        specs += [pl.BlockSpec(part.shape, lambda b, n, _: (0, 0, 0)) for part in far]
        parts += [(len(lefts), 0, planes // 2), (len(lefts), planes // 2, planes)]
    elif far:
        second = at is not None and at * size >= planes // 2
        operands.append(far[second])
        specs.append(block((size, share, depth), planes // 2 // size if second else 0))
        parts.append((len(lefts), 0, size))
    return pl.pallas_call(
        lambda *refs: partial_kernel(parts, *refs),
        out_shape=jax.ShapeDtypeStruct((rows, 3 * channels), jnp.bfloat16),
        grid_spec=pltpu.PrefetchScalarGridSpec(
            num_scalar_prefetch=1,
            grid=(3, count),
            in_specs=specs + [weights, weights],
            out_specs=pl.BlockSpec((rows, width), lambda b, n, _: (0, b * count + n)),
            scratch_shapes=[pltpu.VMEM((size, columns, share, depth), jnp.bfloat16)],
        ),
        compiler_params=pltpu.CompilerParams(
            vmem_limit_bytes=(56 if size == 1 else 36) * 1024 * 1024
        ),
        cost_estimate=pl.CostEstimate(
            flops=2 * rows * depth * 3 * channels,
            bytes_accessed=2 * rows * depth + 6 * depth * channels + 6 * rows * channels,
            transcendentals=0,
        ),
    )(place, *operands, own, other).reshape(size, columns * share, 3 * channels)


def on_device(tokens, gain, in_weight, short_filter, long_filter):
    planes = lax.axis_size("ctx") // CORES
    columns = lax.axis_size("fsdp")
    plane = lax.axis_index("ctx") // CORES
    core = lax.axis_index("ctx") % CORES
    column = lax.axis_index("fsdp")
    early_half = plane < planes // 2
    place = jnp.stack([column, jnp.where(early_half, 0, 1)]).astype(jnp.int32)
    row_count, width = tokens.shape
    long_count = long_filter.shape[0]

    parts = STAGES
    if row_count % (sum(parts) * columns * RIM):
        parts = (1, 1)
    unit = row_count // sum(parts)
    sizes = [unit * part for part in parts]
    stages = [(row_count - sizes[0], sizes[0]), (0, sizes[1])]

    weight = jnp.transpose(in_weight, (1, 0, 2))
    other_weight = lax.ppermute(
        weight,
        "ctx",
        [(p * CORES + c, p * CORES + 1 - c) for p in range(planes) for c in range(CORES)],
    )

    gains = gain.reshape(columns, width)
    gain_here = jnp.stack([pick(gains, column ^ t) for t in range(columns)])[:, None, :]

    def to_trade(stage):
        start, size = stages[stage]
        rows = tokens[start : start + size].reshape(columns, -1, width)
        return [pick(rows, column ^ t) for t in range(columns)]

    def trade(pieces):
        return [swap(piece, columns, t) for t, piece in enumerate(pieces)]

    def normalize(wide):
        wide = jnp.stack(wide).astype(jnp.float32)
        mean_square = jnp.sum(wide * wide, axis=(0, 2), keepdims=True) / (columns * width)
        normed = (wide * lax.rsqrt(mean_square + EPS) * gain_here).astype(jnp.bfloat16)
        return jnp.where(core == 0, normed, jnp.roll(normed, width // 2, axis=2))

    def to_planes(normed, distances):
        rows_of = {}
        for d in distances:
            piece = pick(normed, column ^ ((plane + d) % planes))
            rows_of[planes - d] = plane_shift(piece, [(p, (p + d) % planes) for p in range(planes)])
        return rows_of

    def send_sums(step, terms, arrived, sent=None):
        def onward(term, came):
            if came is None:
                return term
            return (term.astype(jnp.float32) + came.astype(jnp.float32)).astype(jnp.bfloat16)

        right = [(p, p + 1) for p in range(planes - 1) if p < step]
        left = [(p, p - 1) for p in range(1, planes) if p >= planes - step]
        if 2 * step < planes:
            if sent is None:
                sent = jnp.where(early_half, terms[planes - step], terms[step])
            return [plane_shift(onward(sent, arrived[0]), right + left)]
        return [
            plane_shift(onward(terms[planes - step], arrived[0]), right),
            plane_shift(onward(terms[step], arrived[-1]), left),
        ]

    count, steps = len(stages), planes - 1
    order = [m for k in range(1, planes // 2) for m in (planes - k, k)] + [planes // 2, 0]
    around = [planes // 2], [d for d in range(1, planes) if d != planes // 2]
    chains, sums = {}, {}
    normed, rows_of, own, lefts = {}, {}, {}, {}

    def product(stage, size, at):
        return partial_sums(place, *lefts[stage], weight, other_weight, size, at)

    def split(stage, blocks):
        terms = [block for part in blocks for block in part]
        rows = stages[stage][1] // CHAINS[stage]
        chains[stage] = [
            [terms[order.index(m)][part * rows : (part + 1) * rows] for m in range(planes)]
            for part in range(CHAINS[stage])
        ]
        sums[stage] = [[None]] * CHAINS[stage]

    live = {f"pieces{stage}": to_trade(stage) for stage in range(count)}
    for now in range(ROUNDS[-1][-1]):
        fresh = {"weight": other_weight} if now == 0 else {}
        for stage, (to_shares, across, near, far, ready, first) in enumerate(ROUNDS):
            if now < to_shares:
                fresh[f"pieces{stage}"] = live[f"pieces{stage}"]
            if now == to_shares:
                fresh[f"trade{stage}"] = trade(live[f"pieces{stage}"])
            if now == across[0]:
                normed[stage] = normalize(live[f"trade{stage}"])
                rows_of[stage] = {0: pick(normed[stage], column ^ plane)}
            for at, distances in zip(across, around):
                if now == at:
                    fresh[f"planes{stage}{distances[0]}"] = to_planes(normed[stage], distances)
            if now == near:
                own[stage] = jnp.stack([rows_of[stage][m] for m in order])
                fresh[f"near{stage}"] = spread_near(own[stage], columns)
            if now == far:
                fresh[f"near{stage}"] = live[f"near{stage}"]
                fresh[f"far{stage}"] = spread_far(live[f"near{stage}"], columns)
            if now == ready:
                lefts[stage] = [own[stage], *live[f"near{stage}"]], live[f"far{stage}"]
                if now == first:
                    lead = product(stage, 1, None)[0]
                    split(stage, [product(stage, planes, 0)])
                    fresh[f"sums{stage}"] = [send_sums(1, chains[stage][0], [None], lead)]
                else:
                    fresh[f"lead{stage}"] = product(stage, planes // 2, 0)
            if first < now < first + steps:
                fresh[f"sums{stage}"] = [
                    send_sums(now - first + 1, terms, arrived)
                    for terms, arrived in zip(chains[stage], sums[stage])
                ]
        loose = {name: fresh.pop(name) for name in list(fresh) if (name, now) in LOOSE}
        live = together(fresh)
        live.update(loose)
        other_weight = live.pop("weight", other_weight)
        for stage in range(count):
            for distances in around:
                rows_of.get(stage, {}).update(live.pop(f"planes{stage}{distances[0]}", {}))
            if f"sums{stage}" in live:
                sums[stage] = live.pop(f"sums{stage}")

    last = count - 1
    split(last, [live[f"lead{last}"], product(last, planes // 2, 1)])
    for step in range(1, planes):
        sums[last] = [
            send_sums(step, terms, arrived) for terms, arrived in zip(chains[last], sums[last])
        ]

    def summed(stage):
        parts = []
        for terms, arrived in zip(chains[stage], sums[stage]):
            total = terms[0].astype(jnp.float32)
            total = total + arrived[0].astype(jnp.float32) + arrived[-1].astype(jnp.float32)
            parts.append(total.astype(jnp.bfloat16))
        return parts

    (last_rows,) = summed(0)
    rims = passed_rims(last_rows, short_filter, long_count)
    projected = jnp.concatenate([*summed(1), last_rows], axis=0)
    return finish(projected, rims, short_filter, long_filter)


def solution(mesh):
    return jax.shard_map(
        on_device,
        mesh=mesh,
        in_specs=(
            P("ctx", "fsdp"),
            P(),
            P("ctx", None, "fsdp"),
            P(None, None, "fsdp"),
            P(None, "fsdp"),
        ),
        out_specs=P("ctx", "fsdp"),
        check_vma=False,
    )
```

```python
import jax
import jax.numpy as jnp
import numpy as np
from jax import lax
from jax.experimental import pallas as pl
from jax.experimental.pallas import tpu as pltpu
from jax.sharding import PartitionSpec as P

CORES = 2
EPS = 1e-06
STAGES = (3, 5)
ROUNDS = ((0, (1, 1), 2, 3, 4, 4), (1, (2, 3), 4, 5, 6, 7))
LOOSE = (("planes12", 2), ("near0", 2), ("near1", 4), ("sums0", 4))
CHAINS = (1, 1)
RIM = 16


def pick(stack, index):
    return lax.dynamic_index_in_dim(stack, index, 0, keepdims=False)


def swap(value, count, bits):
    if bits == 0:
        return value
    return lax.ppermute(value, "fsdp", [(j, j ^ bits) for j in range(count)])


def plane_shift(value, edges):
    return lax.ppermute(
        value, "ctx", [(a * CORES + c, b * CORES + c) for a, b in edges for c in range(CORES)]
    )


def dft_matrices(length):
    half = length // 2
    k = np.concatenate([np.arange(half), [half], np.arange(1, half)])[:, None]
    angle = 2.0 * np.pi * ((k * np.arange(length)[None, :]) % length) / length
    wave = np.where(np.arange(length)[:, None] <= half, np.cos(angle), -np.sin(angle))
    weight = np.where((k == 0) | (k == half), 1.0, 2.0) / length
    return wave.astype(np.float32), (weight * wave)[:, half:].T.astype(np.float32)


def halves(value):
    high = value.astype(jnp.bfloat16)
    return high, (value - high.astype(jnp.float32)).astype(jnp.bfloat16)


def dot(a, b):
    return jnp.dot(a, b, preferred_element_type=jnp.float32)


def finish_kernel(
    query, key, value, rims, short, long, analysis, synthesis, out, extended, signal
):
    row_count = out.shape[0]
    taps = long.shape[0]
    length = 2 * taps
    reach = short.shape[0]
    for b, body in enumerate((query, key, value)):
        extended[b, :8] = rims[taps + RIM * b : taps + RIM * (b + 1)].astype(jnp.float32)[RIM - 8 :]
        extended[b, 8:] = body[...].astype(jnp.float32)

    def featurized(b, start, count):
        result = None
        for s in range(reach):
            term = short[s, b : b + 1, :] * extended[b, 8 + start - s : 8 + start - s + count]
            result = term if result is None else result + term
        return result

    signal[:taps] = rims[:taps]
    for start in range(0, row_count, taps):
        gated = featurized(1, start, taps) * featurized(2, start, taps)
        signal[taps + start : 2 * taps + start] = gated.astype(jnp.bfloat16)

    def both(product):
        return product[: product.shape[0] // 2] + product[product.shape[0] // 2 :]

    long_high, long_low = halves(long[...])
    tones = both(dot(analysis[:, :taps], long_high)) + dot(analysis[:length, :taps], long_low)
    first = lax.broadcasted_iota(jnp.int32, (taps, tones.shape[1]), 0) == 0
    real_tones = tones[:taps]
    cross_tones = jnp.where(first, 0.0, tones[taps:])
    last_tones = jnp.where(first, tones[taps:], tones[:taps])
    for start in range(0, row_count, taps):
        spectrum = both(dot(analysis[...], signal[start : start + length]))
        real, imag = spectrum[:taps], spectrum[taps:]
        high, low = halves(
            jnp.concatenate(
                [
                    real * real_tones - imag * cross_tones,
                    real * cross_tones + imag * last_tones,
                ],
                axis=0,
            )
        )
        response = both(dot(synthesis[...], high)) + dot(synthesis[:taps], low)
        out[start : start + taps] = (featurized(0, start, taps) * response).astype(out.dtype)


def finish(projected, rims, short_filter, long_filter):
    row_count = projected.shape[0]
    taps, channels = long_filter.shape
    constants = [
        jnp.concatenate(halves(jnp.asarray(matrix)), axis=0) for matrix in dft_matrices(2 * taps)
    ]

    def branch(b):
        return pl.BlockSpec((row_count, channels), lambda i: (0, b))

    operands = [*[projected] * 3, rims, short_filter, long_filter, *constants]
    specs = (
        [branch(b) for b in range(3)]
        + [
            pl.BlockSpec(rims.shape, lambda i: (0, 0)),
            pl.BlockSpec(short_filter.shape, lambda i: (0, 0, 0)),
            pl.BlockSpec(long_filter.shape, lambda i: (0, 0)),
        ]
        + [pl.BlockSpec(m.shape, lambda i: (0, 0)) for m in constants]
    )
    return pl.pallas_call(
        finish_kernel,
        out_shape=jax.ShapeDtypeStruct((row_count, channels), jnp.bfloat16),
        grid=(1,),
        in_specs=specs,
        out_specs=pl.BlockSpec((row_count, channels), lambda i: (0, 0)),
        scratch_shapes=[
            pltpu.VMEM((3, 8 + row_count, channels), jnp.float32),
            pltpu.VMEM((taps + row_count, channels), jnp.bfloat16),
        ],
        compiler_params=pltpu.CompilerParams(vmem_limit_bytes=32 * 1024 * 1024),
        cost_estimate=pl.CostEstimate(
            flops=row_count * channels * 5000, bytes_accessed=row_count * channels * 10, transcendentals=0
        ),
    )(*operands)


def passed_rims(last_rows, short_filter, long_count):
    reach = short_filter.shape[0]
    channels = short_filter.shape[2]
    total = last_rows.shape[0]
    branches = [last_rows[:, b * channels : (b + 1) * channels] for b in range(3)]
    mixed = []
    for b in (1, 2):
        rows = branches[b].astype(jnp.float32)
        mixed.append(
            sum(
                short_filter[s, b] * rows[total - long_count - s : total - s] for s in range(reach)
            )
        )
    gated = (mixed[0] * mixed[1]).astype(jnp.bfloat16)
    packed = jnp.concatenate([gated] + [rows[total - RIM :] for rows in branches], axis=0)
    count = lax.axis_size("ctx")
    return lax.ppermute(packed, "ctx", [(i, i + 1) for i in range(count - 1)])


def together(values):
    leaves, tree = jax.tree.flatten(values)
    anywhere = pl.BlockSpec(memory_space=pl.ANY)
    leaves = pl.pallas_call(
        lambda *refs: None,
        out_shape=[jax.ShapeDtypeStruct(leaf.shape, leaf.dtype) for leaf in leaves],
        in_specs=[anywhere] * len(leaves),
        out_specs=[anywhere] * len(leaves),
        input_output_aliases={at: at for at in range(len(leaves))},
    )(*leaves)
    return jax.tree.unflatten(tree, leaves)


def spread_near(value, columns):
    if columns != 4:
        return [swap(value, columns, t) for t in range(1, columns)]
    return [swap(value, columns, 1), swap(value, columns, 2)]


def spread_far(near, columns):
    if columns != 4:
        return []
    half = near[0].shape[0] // 2
    return [swap(near[1][:half], columns, 1), swap(near[0][half:], columns, 2)]


def partial_kernel(parts, place, *refs):
    *lefts, own, other, out, joined = refs
    size, columns, share, depth = joined.shape

    @pl.when((pl.program_id(0) == 0) & (pl.program_id(1) == 0))
    def _():
        for (t, begin, end), left in zip(parts, lefts):
            joined[begin:end, place[0] ^ t] = left[...]

    rows = joined[...].reshape(size * columns * share, depth)
    half = depth // 2
    total = dot(rows[:, :half], own[0]) + dot(rows[:, half:], other[0])
    out[...] = total.astype(out.dtype)


def partial_sums(place, lefts, far, own, other, size, at):
    planes, share, depth = lefts[0].shape
    columns = len(lefts) + (1 if far else 0)
    channels = own.shape[2]
    rows = size * columns * share
    width = channels
    count = channels // width
    weights = pl.BlockSpec((1, own.shape[1], width), lambda b, n, _: (b, 0, n))

    def block(shape, before=0):
        return pl.BlockSpec(
            shape, lambda b, n, place: (place[1] if at is None else at - before, 0, 0)
        )

    operands = list(lefts)
    specs = [block((size, share, depth)) for _ in lefts]
    parts = [(t, 0, size) for t in range(len(lefts))]
    if far and size == planes:
        operands += far
        specs += [pl.BlockSpec(part.shape, lambda b, n, _: (0, 0, 0)) for part in far]
        parts += [(len(lefts), 0, planes // 2), (len(lefts), planes // 2, planes)]
    elif far:
        second = at is not None and at * size >= planes // 2
        operands.append(far[second])
        specs.append(block((size, share, depth), planes // 2 // size if second else 0))
        parts.append((len(lefts), 0, size))
    return pl.pallas_call(
        lambda *refs: partial_kernel(parts, *refs),
        out_shape=jax.ShapeDtypeStruct((rows, 3 * channels), jnp.bfloat16),
        grid_spec=pltpu.PrefetchScalarGridSpec(
            num_scalar_prefetch=1,
            grid=(3, count),
            in_specs=specs + [weights, weights],
            out_specs=pl.BlockSpec((rows, width), lambda b, n, _: (0, b * count + n)),
            scratch_shapes=[pltpu.VMEM((size, columns, share, depth), jnp.bfloat16)],
        ),
        compiler_params=pltpu.CompilerParams(
            vmem_limit_bytes=(56 if size == 1 else 36) * 1024 * 1024
        ),
        cost_estimate=pl.CostEstimate(
            flops=2 * rows * depth * 3 * channels,
            bytes_accessed=2 * rows * depth + 6 * depth * channels + 6 * rows * channels,
            transcendentals=0,
        ),
    )(place, *operands, own, other).reshape(size, columns * share, 3 * channels)


def on_device(tokens, gain, in_weight, short_filter, long_filter):
    planes = lax.axis_size("ctx") // CORES
    columns = lax.axis_size("fsdp")
    plane = lax.axis_index("ctx") // CORES
    core = lax.axis_index("ctx") % CORES
    column = lax.axis_index("fsdp")
    early_half = plane < planes // 2
    place = jnp.stack([column, jnp.where(early_half, 0, 1)]).astype(jnp.int32)
    row_count, width = tokens.shape
    long_count = long_filter.shape[0]

    parts = STAGES
    if row_count % (sum(parts) * columns * RIM):
        parts = (1, 1)
    unit = row_count // sum(parts)
    sizes = [unit * part for part in parts]
    stages = [(row_count - sizes[0], sizes[0]), (0, sizes[1])]

    weight = jnp.transpose(in_weight, (1, 0, 2))
    other_weight = lax.ppermute(
        weight,
        "ctx",
        [(p * CORES + c, p * CORES + 1 - c) for p in range(planes) for c in range(CORES)],
    )

    gains = gain.reshape(columns, width)
    gain_here = jnp.stack([pick(gains, column ^ t) for t in range(columns)])[:, None, :]

    def to_trade(stage):
        start, size = stages[stage]
        rows = tokens[start : start + size].reshape(columns, -1, width)
        return [pick(rows, column ^ t) for t in range(columns)]

    def trade(pieces):
        return [swap(piece, columns, t) for t, piece in enumerate(pieces)]

    def normalize(wide):
        wide = jnp.stack(wide).astype(jnp.float32)
        mean_square = jnp.sum(wide * wide, axis=(0, 2), keepdims=True) / (columns * width)
        normed = (wide * lax.rsqrt(mean_square + EPS) * gain_here).astype(jnp.bfloat16)
        return jnp.where(core == 0, normed, jnp.roll(normed, width // 2, axis=2))

    def to_planes(normed, distances):
        rows_of = {}
        for d in distances:
            piece = pick(normed, column ^ ((plane + d) % planes))
            rows_of[planes - d] = plane_shift(piece, [(p, (p + d) % planes) for p in range(planes)])
        return rows_of

    def send_sums(step, terms, arrived, sent=None):
        def onward(term, came):
            if came is None:
                return term
            return (term.astype(jnp.float32) + came.astype(jnp.float32)).astype(jnp.bfloat16)

        right = [(p, p + 1) for p in range(planes - 1) if p < step]
        left = [(p, p - 1) for p in range(1, planes) if p >= planes - step]
        if 2 * step < planes:
            if sent is None:
                sent = jnp.where(early_half, terms[planes - step], terms[step])
            return [plane_shift(onward(sent, arrived[0]), right + left)]
        return [
            plane_shift(onward(terms[planes - step], arrived[0]), right),
            plane_shift(onward(terms[step], arrived[-1]), left),
        ]

    count, steps = len(stages), planes - 1
    order = [m for k in range(1, planes // 2) for m in (planes - k, k)] + [planes // 2, 0]
    around = [planes // 2], [d for d in range(1, planes) if d != planes // 2]
    chains, sums = {}, {}
    normed, rows_of, own, lefts = {}, {}, {}, {}

    def product(stage, size, at):
        return partial_sums(place, *lefts[stage], weight, other_weight, size, at)

    def split(stage, blocks):
        terms = [block for part in blocks for block in part]
        rows = stages[stage][1] // CHAINS[stage]
        chains[stage] = [
            [terms[order.index(m)][part * rows : (part + 1) * rows] for m in range(planes)]
            for part in range(CHAINS[stage])
        ]
        sums[stage] = [[None]] * CHAINS[stage]

    live = {f"pieces{stage}": to_trade(stage) for stage in range(count)}
    for now in range(ROUNDS[-1][-1]):
        fresh = {"weight": other_weight} if now == 0 else {}
        for stage, (to_shares, across, near, far, ready, first) in enumerate(ROUNDS):
            if now < to_shares:
                fresh[f"pieces{stage}"] = live[f"pieces{stage}"]
            if now == to_shares:
                fresh[f"trade{stage}"] = trade(live[f"pieces{stage}"])
            if now == across[0]:
                normed[stage] = normalize(live[f"trade{stage}"])
                rows_of[stage] = {0: pick(normed[stage], column ^ plane)}
            for at, distances in zip(across, around):
                if now == at:
                    fresh[f"planes{stage}{distances[0]}"] = to_planes(normed[stage], distances)
            if now == near:
                own[stage] = jnp.stack([rows_of[stage][m] for m in order])
                fresh[f"near{stage}"] = spread_near(own[stage], columns)
            if now == far:
                fresh[f"near{stage}"] = live[f"near{stage}"]
                fresh[f"far{stage}"] = spread_far(live[f"near{stage}"], columns)
            if now == ready:
                lefts[stage] = [own[stage], *live[f"near{stage}"]], live[f"far{stage}"]
                if now == first:
                    lead = product(stage, 1, None)[0]
                    split(stage, [product(stage, planes, 0)])
                    fresh[f"sums{stage}"] = [send_sums(1, chains[stage][0], [None], lead)]
                else:
                    fresh[f"lead{stage}"] = product(stage, planes // 2, 0)
            if first < now < first + steps:
                fresh[f"sums{stage}"] = [
                    send_sums(now - first + 1, terms, arrived)
                    for terms, arrived in zip(chains[stage], sums[stage])
                ]
        loose = {name: fresh.pop(name) for name in list(fresh) if (name, now) in LOOSE}
        live = together(fresh)
        live.update(loose)
        other_weight = live.pop("weight", other_weight)
        for stage in range(count):
            for distances in around:
                rows_of.get(stage, {}).update(live.pop(f"planes{stage}{distances[0]}", {}))
            if f"sums{stage}" in live:
                sums[stage] = live.pop(f"sums{stage}")

    last = count - 1
    split(last, [live[f"lead{last}"], product(last, planes // 2, 1)])
    for step in range(1, planes):
        sums[last] = [
            send_sums(step, terms, arrived) for terms, arrived in zip(chains[last], sums[last])
        ]

    def summed(stage):
        parts = []
        for terms, arrived in zip(chains[stage], sums[stage]):
            total = terms[0].astype(jnp.float32)
            total = total + arrived[0].astype(jnp.float32) + arrived[-1].astype(jnp.float32)
            parts.append(total.astype(jnp.bfloat16))
        return parts

    (last_rows,) = summed(0)
    rims = passed_rims(last_rows, short_filter, long_count)
    projected = jnp.concatenate([*summed(1), last_rows], axis=0)
    return finish(projected, rims, short_filter, long_filter)


def solution(mesh):
    return jax.shard_map(
        on_device,
        mesh=mesh,
        in_specs=(
            P("ctx", "fsdp"),
            P(),
            P("ctx", None, "fsdp"),
            P(None, None, "fsdp"),
            P(None, "fsdp"),
        ),
        out_specs=P("ctx", "fsdp"),
        check_vma=False,
    )
```

```python
import jax
import jax.numpy as jnp
import numpy as np
from jax import lax
from jax.experimental import pallas as pl
from jax.experimental.pallas import tpu as pltpu
from jax.sharding import PartitionSpec as P

CORES = 2
EPS = 1e-06
STAGES = (3, 5)
ROUNDS = ((0, (1, 1), 2, 3, 4, 4), (1, (2, 3), 4, 5, 6, 7))
LOOSE = (("planes12", 2), ("near0", 2), ("near1", 4), ("sums0", 4))
CHAINS = (1, 1)
RIM = 16


def pick(stack, index):
    return lax.dynamic_index_in_dim(stack, index, 0, keepdims=False)


def swap(value, count, bits):
    if bits == 0:
        return value
    return lax.ppermute(value, "fsdp", [(j, j ^ bits) for j in range(count)])


def plane_shift(value, edges):
    return lax.ppermute(
        value, "ctx", [(a * CORES + c, b * CORES + c) for a, b in edges for c in range(CORES)]
    )


def dft_matrices(length):
    half = length // 2
    k = np.concatenate([np.arange(half), [half], np.arange(1, half)])[:, None]
    angle = 2.0 * np.pi * ((k * np.arange(length)[None, :]) % length) / length
    wave = np.where(np.arange(length)[:, None] <= half, np.cos(angle), -np.sin(angle))
    weight = np.where((k == 0) | (k == half), 1.0, 2.0) / length
    return wave.astype(np.float32), (weight * wave)[:, half:].T.astype(np.float32)


def halves(value):
    high = value.astype(jnp.bfloat16)
    return high, (value - high.astype(jnp.float32)).astype(jnp.bfloat16)


def dot(a, b):
    return jnp.dot(a, b, preferred_element_type=jnp.float32)


def finish_kernel(
    query, key, value, rims, short, long, analysis, synthesis, out, extended, signal
):
    row_count = out.shape[0]
    taps = long.shape[0]
    length = 2 * taps
    reach = short.shape[0]
    for b, body in enumerate((query, key, value)):
        extended[b, :8] = rims[taps + RIM * b : taps + RIM * (b + 1)].astype(jnp.float32)[RIM - 8 :]
        extended[b, 8:] = body[...].astype(jnp.float32)

    def featurized(b, start, count):
        result = None
        for s in range(reach):
            term = short[s, b : b + 1, :] * extended[b, 8 + start - s : 8 + start - s + count]
            result = term if result is None else result + term
        return result

    signal[:taps] = rims[:taps]
    for start in range(0, row_count, taps):
        gated = featurized(1, start, taps) * featurized(2, start, taps)
        signal[taps + start : 2 * taps + start] = gated.astype(jnp.bfloat16)

    def both(product):
        return product[: product.shape[0] // 2] + product[product.shape[0] // 2 :]

    long_high, long_low = halves(long[...])
    tones = both(dot(analysis[:, :taps], long_high)) + dot(analysis[:length, :taps], long_low)
    first = lax.broadcasted_iota(jnp.int32, (taps, tones.shape[1]), 0) == 0
    real_tones = tones[:taps]
    cross_tones = jnp.where(first, 0.0, tones[taps:])
    last_tones = jnp.where(first, tones[taps:], tones[:taps])
    for start in range(0, row_count, taps):
        spectrum = both(dot(analysis[...], signal[start : start + length]))
        real, imag = spectrum[:taps], spectrum[taps:]
        high, low = halves(
            jnp.concatenate(
                [
                    real * real_tones - imag * cross_tones,
                    real * cross_tones + imag * last_tones,
                ],
                axis=0,
            )
        )
        response = both(dot(synthesis[...], high)) + dot(synthesis[:taps], low)
        out[start : start + taps] = (featurized(0, start, taps) * response).astype(out.dtype)


def finish(projected, rims, short_filter, long_filter):
    row_count = projected.shape[0]
    taps, channels = long_filter.shape
    constants = [
        jnp.concatenate(halves(jnp.asarray(matrix)), axis=0) for matrix in dft_matrices(2 * taps)
    ]

    def branch(b):
        return pl.BlockSpec((row_count, channels), lambda i: (0, b))

    operands = [*[projected] * 3, rims, short_filter, long_filter, *constants]
    specs = (
        [branch(b) for b in range(3)]
        + [
            pl.BlockSpec(rims.shape, lambda i: (0, 0)),
            pl.BlockSpec(short_filter.shape, lambda i: (0, 0, 0)),
            pl.BlockSpec(long_filter.shape, lambda i: (0, 0)),
        ]
        + [pl.BlockSpec(m.shape, lambda i: (0, 0)) for m in constants]
    )
    return pl.pallas_call(
        finish_kernel,
        out_shape=jax.ShapeDtypeStruct((row_count, channels), jnp.bfloat16),
        grid=(1,),
        in_specs=specs,
        out_specs=pl.BlockSpec((row_count, channels), lambda i: (0, 0)),
        scratch_shapes=[
            pltpu.VMEM((3, 8 + row_count, channels), jnp.float32),
            pltpu.VMEM((taps + row_count, channels), jnp.bfloat16),
        ],
        compiler_params=pltpu.CompilerParams(vmem_limit_bytes=32 * 1024 * 1024),
        cost_estimate=pl.CostEstimate(
            flops=row_count * channels * 5000, bytes_accessed=row_count * channels * 10, transcendentals=0
        ),
    )(*operands)


def passed_rims(last_rows, short_filter, long_count):
    reach = short_filter.shape[0]
    channels = short_filter.shape[2]
    total = last_rows.shape[0]
    branches = [last_rows[:, b * channels : (b + 1) * channels] for b in range(3)]
    mixed = []
    for b in (1, 2):
        rows = branches[b].astype(jnp.float32)
        mixed.append(
            sum(
                short_filter[s, b] * rows[total - long_count - s : total - s] for s in range(reach)
            )
        )
    gated = (mixed[0] * mixed[1]).astype(jnp.bfloat16)
    packed = jnp.concatenate([gated] + [rows[total - RIM :] for rows in branches], axis=0)
    count = lax.axis_size("ctx")
    return lax.ppermute(packed, "ctx", [(i, i + 1) for i in range(count - 1)])


def together(values):
    leaves, tree = jax.tree.flatten(values)
    anywhere = pl.BlockSpec(memory_space=pl.ANY)
    leaves = pl.pallas_call(
        lambda *refs: None,
        out_shape=[jax.ShapeDtypeStruct(leaf.shape, leaf.dtype) for leaf in leaves],
        in_specs=[anywhere] * len(leaves),
        out_specs=[anywhere] * len(leaves),
        input_output_aliases={at: at for at in range(len(leaves))},
    )(*leaves)
    return jax.tree.unflatten(tree, leaves)


def spread_near(value, columns):
    if columns != 4:
        return [swap(value, columns, t) for t in range(1, columns)]
    return [swap(value, columns, 1), swap(value, columns, 2)]


def spread_far(near, columns):
    if columns != 4:
        return []
    half = near[0].shape[0] // 2
    return [swap(near[1][:half], columns, 1), swap(near[0][half:], columns, 2)]


def partial_kernel(parts, place, *refs):
    *lefts, own, other, out, joined = refs
    size, columns, share, depth = joined.shape

    @pl.when((pl.program_id(0) == 0) & (pl.program_id(1) == 0))
    def _():
        for (t, begin, end), left in zip(parts, lefts):
            joined[begin:end, place[0] ^ t] = left[...]

    rows = joined[...].reshape(size * columns * share, depth)
    half = depth // 2
    total = dot(rows[:, :half], own[0]) + dot(rows[:, half:], other[0])
    out[...] = total.astype(out.dtype)


def partial_sums(place, lefts, far, own, other, size, at):
    planes, share, depth = lefts[0].shape
    columns = len(lefts) + (1 if far else 0)
    channels = own.shape[2]
    rows = size * columns * share
    width = channels
    count = channels // width
    weights = pl.BlockSpec((1, own.shape[1], width), lambda b, n, _: (b, 0, n))

    def block(shape, before=0):
        return pl.BlockSpec(
            shape, lambda b, n, place: (place[1] if at is None else at - before, 0, 0)
        )

    operands = list(lefts)
    specs = [block((size, share, depth)) for _ in lefts]
    parts = [(t, 0, size) for t in range(len(lefts))]
    if far and size == planes:
        operands += far
        specs += [pl.BlockSpec(part.shape, lambda b, n, _: (0, 0, 0)) for part in far]
        parts += [(len(lefts), 0, planes // 2), (len(lefts), planes // 2, planes)]
    elif far:
        second = at is not None and at * size >= planes // 2
        operands.append(far[second])
        specs.append(block((size, share, depth), planes // 2 // size if second else 0))
        parts.append((len(lefts), 0, size))
    return pl.pallas_call(
        lambda *refs: partial_kernel(parts, *refs),
        out_shape=jax.ShapeDtypeStruct((rows, 3 * channels), jnp.bfloat16),
        grid_spec=pltpu.PrefetchScalarGridSpec(
            num_scalar_prefetch=1,
            grid=(3, count),
            in_specs=specs + [weights, weights],
            out_specs=pl.BlockSpec((rows, width), lambda b, n, _: (0, b * count + n)),
            scratch_shapes=[pltpu.VMEM((size, columns, share, depth), jnp.bfloat16)],
        ),
        compiler_params=pltpu.CompilerParams(
            vmem_limit_bytes=(56 if size == 1 else 36) * 1024 * 1024
        ),
        cost_estimate=pl.CostEstimate(
            flops=2 * rows * depth * 3 * channels,
            bytes_accessed=2 * rows * depth + 6 * depth * channels + 6 * rows * channels,
            transcendentals=0,
        ),
    )(place, *operands, own, other).reshape(size, columns * share, 3 * channels)


def on_device(tokens, gain, in_weight, short_filter, long_filter):
    planes = lax.axis_size("ctx") // CORES
    columns = lax.axis_size("fsdp")
    plane = lax.axis_index("ctx") // CORES
    core = lax.axis_index("ctx") % CORES
    column = lax.axis_index("fsdp")
    early_half = plane < planes // 2
    place = jnp.stack([column, jnp.where(early_half, 0, 1)]).astype(jnp.int32)
    row_count, width = tokens.shape
    long_count = long_filter.shape[0]

    parts = STAGES
    if row_count % (sum(parts) * columns * RIM):
        parts = (1, 1)
    unit = row_count // sum(parts)
    sizes = [unit * part for part in parts]
    stages = [(row_count - sizes[0], sizes[0]), (0, sizes[1])]

    weight = jnp.transpose(in_weight, (1, 0, 2))
    other_weight = lax.ppermute(
        weight,
        "ctx",
        [(p * CORES + c, p * CORES + 1 - c) for p in range(planes) for c in range(CORES)],
    )

    gains = gain.reshape(columns, width)
    gain_here = jnp.stack([pick(gains, column ^ t) for t in range(columns)])[:, None, :]

    def to_trade(stage):
        start, size = stages[stage]
        rows = tokens[start : start + size].reshape(columns, -1, width)
        return [pick(rows, column ^ t) for t in range(columns)]

    def trade(pieces):
        return [swap(piece, columns, t) for t, piece in enumerate(pieces)]

    def normalize(wide):
        wide = jnp.stack(wide).astype(jnp.float32)
        mean_square = jnp.sum(wide * wide, axis=(0, 2), keepdims=True) / (columns * width)
        normed = (wide * lax.rsqrt(mean_square + EPS) * gain_here).astype(jnp.bfloat16)
        return jnp.where(core == 0, normed, jnp.roll(normed, width // 2, axis=2))

    def to_planes(normed, distances):
        rows_of = {}
        for d in distances:
            piece = pick(normed, column ^ ((plane + d) % planes))
            rows_of[planes - d] = plane_shift(piece, [(p, (p + d) % planes) for p in range(planes)])
        return rows_of

    def send_sums(step, terms, arrived, sent=None):
        def onward(term, came):
            if came is None:
                return term
            return (term.astype(jnp.float32) + came.astype(jnp.float32)).astype(jnp.bfloat16)

        right = [(p, p + 1) for p in range(planes - 1) if p < step]
        left = [(p, p - 1) for p in range(1, planes) if p >= planes - step]
        if 2 * step < planes:
            if sent is None:
                sent = jnp.where(early_half, terms[planes - step], terms[step])
            return [plane_shift(onward(sent, arrived[0]), right + left)]
        return [
            plane_shift(onward(terms[planes - step], arrived[0]), right),
            plane_shift(onward(terms[step], arrived[-1]), left),
        ]

    count, steps = len(stages), planes - 1
    order = [m for k in range(1, planes // 2) for m in (planes - k, k)] + [planes // 2, 0]
    around = [planes // 2], [d for d in range(1, planes) if d != planes // 2]
    chains, sums = {}, {}
    normed, rows_of, own, lefts = {}, {}, {}, {}

    def product(stage, size, at):
        return partial_sums(place, *lefts[stage], weight, other_weight, size, at)

    def split(stage, blocks):
        terms = [block for part in blocks for block in part]
        rows = stages[stage][1] // CHAINS[stage]
        chains[stage] = [
            [terms[order.index(m)][part * rows : (part + 1) * rows] for m in range(planes)]
            for part in range(CHAINS[stage])
        ]
        sums[stage] = [[None]] * CHAINS[stage]

    live = {f"pieces{stage}": to_trade(stage) for stage in range(count)}
    for now in range(ROUNDS[-1][-1]):
        fresh = {"weight": other_weight} if now == 0 else {}
        for stage, (to_shares, across, near, far, ready, first) in enumerate(ROUNDS):
            if now < to_shares:
                fresh[f"pieces{stage}"] = live[f"pieces{stage}"]
            if now == to_shares:
                fresh[f"trade{stage}"] = trade(live[f"pieces{stage}"])
            if now == across[0]:
                normed[stage] = normalize(live[f"trade{stage}"])
                rows_of[stage] = {0: pick(normed[stage], column ^ plane)}
            for at, distances in zip(across, around):
                if now == at:
                    fresh[f"planes{stage}{distances[0]}"] = to_planes(normed[stage], distances)
            if now == near:
                own[stage] = jnp.stack([rows_of[stage][m] for m in order])
                fresh[f"near{stage}"] = spread_near(own[stage], columns)
            if now == far:
                fresh[f"near{stage}"] = live[f"near{stage}"]
                fresh[f"far{stage}"] = spread_far(live[f"near{stage}"], columns)
            if now == ready:
                lefts[stage] = [own[stage], *live[f"near{stage}"]], live[f"far{stage}"]
                if now == first:
                    lead = product(stage, 1, None)[0]
                    split(stage, [product(stage, planes, 0)])
                    fresh[f"sums{stage}"] = [send_sums(1, chains[stage][0], [None], lead)]
                else:
                    fresh[f"lead{stage}"] = product(stage, 1, None)
            if first < now < first + steps:
                fresh[f"sums{stage}"] = [
                    send_sums(now - first + 1, terms, arrived)
                    for terms, arrived in zip(chains[stage], sums[stage])
                ]
        loose = {name: fresh.pop(name) for name in list(fresh) if (name, now) in LOOSE}
        live = together(fresh)
        live.update(loose)
        other_weight = live.pop("weight", other_weight)
        for stage in range(count):
            for distances in around:
                rows_of.get(stage, {}).update(live.pop(f"planes{stage}{distances[0]}", {}))
            if f"sums{stage}" in live:
                sums[stage] = live.pop(f"sums{stage}")

    last = count - 1
    split(last, [product(last, planes, 0)])
    leads = jnp.split(live[f"lead{last}"][0], CHAINS[last], axis=0)
    for step in range(1, planes):
        sums[last] = [
            send_sums(step, terms, arrived, lead if step == 1 else None)
            for terms, arrived, lead in zip(chains[last], sums[last], leads)
        ]

    def summed(stage):
        parts = []
        for terms, arrived in zip(chains[stage], sums[stage]):
            total = terms[0].astype(jnp.float32)
            total = total + arrived[0].astype(jnp.float32) + arrived[-1].astype(jnp.float32)
            parts.append(total.astype(jnp.bfloat16))
        return parts

    (last_rows,) = summed(0)
    rims = passed_rims(last_rows, short_filter, long_count)
    projected = jnp.concatenate([*summed(1), last_rows], axis=0)
    return finish(projected, rims, short_filter, long_filter)


def solution(mesh):
    return jax.shard_map(
        on_device,
        mesh=mesh,
        in_specs=(
            P("ctx", "fsdp"),
            P(),
            P("ctx", None, "fsdp"),
            P(None, None, "fsdp"),
            P(None, "fsdp"),
        ),
        out_specs=P("ctx", "fsdp"),
        check_vma=False,
    )
```
